256 devices in a mesh: seq: 32 (over z, x), tensor: 4 (over y), dp: 2 (over core).
Axes of the slice: x: 4, y: 4, z: 8, core: 2. Of those that a mesh axis runs over, the one named last changes fastest.
Arguments:
- queries: bfloat16 [32768, 4096], P(('dp', 'seq'), 'tensor'), parts along dimension 0, may hold values from -41 to 41
- database: bfloat16 [512, 128, 1024], P('seq'), may hold values from -36 to 36
- nbr_ids: int32 [512, 2], P(('dp', 'seq')), parts along dimension 0, may hold values from 0 to 511, as said below
- norm_gain: bfloat16 [1024], replicated, may hold values from 0.25 to 1.75
- enc_qkv: bfloat16 [3, 1024, 1024], P(None, None, 'tensor'), may hold values from -2.6 to 2.6
- enc_out: bfloat16 [1024, 1024], P('tensor'), may hold values from -0.75 to 0.75
- out_gain: bfloat16 [1024], replicated, may hold values from 0.25 to 1.75
- cca_kv: bfloat16 [2, 1024, 4096], P(None, None, 'tensor'), may hold values from -0.1875 to 0.1875
Outputs:
- attended: bfloat16 [32768, 4096], P(('dp', 'seq'), 'tensor'), parts along dimension 0
The draws below stay inside these ranges and needn't reach their ends.
There are 2 independent parts, one for each index of `dp`. The reference program is written for one: setup_inputs(seed, part) draws one part's arguments, and reference() takes and returns one part's arrays. A program takes and returns all parts, laid end to end along the dimension named above; an argument that names none is the same for every part. Nothing has to cross between parts.
Inputs may be any that keep to these rules, and one draw needn't show every extreme that they name: `nbr_ids`: block id b lies in database shard b // 16, held by index b // 16 of seq. The 16 ids of one index of seq are distinct and at most 2 of them lie in one shard; in every draw one shard holds exactly 2 of the ids of every index of seq.
All inputs are finite; a program needn't handle non-finite values.
Results may differ from the reference program's by a relative error of at most 0.039.
Values may be sent and summed in bfloat16 or wider, within the bound.
A program may use at most 128 MiB of HBM per device.

```python
import math
import jax
import jax.numpy as jnp
from jax import lax

DE = 1024
HDE = 64
HD = 128
M = 64
R = 128
K = 2
BLOCKS_DEV = 16
QW = 4096
WINDOWS_DEV = 8
TOKENS = 16384
WINDOWS = 256
DB_BLOCKS = 512
CAP = 2
N_SEQ = 32
N_TENSOR = 4


def draw_database(key, part):
    key = jax.random.fold_in(key, 11)
    key_base, key_rows, key_cols = jax.random.split(key, 3)
    full_shape = (DB_BLOCKS, R, DE)
    col_scale = jnp.exp(jax.random.uniform(key_cols, (1, 1, DE), jnp.float32, -1.2, 1.1))
    base_draw = jax.random.truncated_normal(key_base, -4.0, 4.0, full_shape, jnp.float32)
    row_scale = jnp.exp(jax.random.uniform(key_rows, (DB_BLOCKS, R, 1), jnp.float32, -1.2, 1.1))
    values = base_draw * row_scale * col_scale
    return values.astype(jnp.bfloat16)


def draw_queries(key, part):
    key = jax.random.fold_in(key, 12)
    key_base = jax.random.fold_in(key, 0)
    full_shape = (TOKENS, QW)
    values = jax.random.truncated_normal(key_base, -5.0, 5.0, full_shape, jnp.float32)
    return values.astype(jnp.bfloat16)


def draw_enc_qkv(key, part):
    key = jax.random.fold_in(key, 13)
    key_base = jax.random.fold_in(key, 0)
    full_shape = (3, DE, DE)
    values = jax.random.truncated_normal(key_base, -4.0, 4.0, full_shape, jnp.float32) / math.sqrt(DE)
    return values.astype(jnp.bfloat16)


def draw_nbr_ids(key, part):
    key = jax.random.fold_in(key, 14)
    key_noise, key_level, key_full, key_order, key_offset = jax.random.split(key, 5)
    request_count = WINDOWS_DEV * K
    slot_count = N_SEQ * CAP
    slot_ids = jnp.arange(slot_count, dtype=jnp.int32)
    slot_shard = slot_ids // CAP
    noise_score = jax.random.randint(key_noise, (N_SEQ, slot_count), 0, 2 ** 16, jnp.int32)
    shard_level = jax.random.randint(key_level, (N_SEQ,), 0, 4, jnp.int32)
    full_shard = jax.random.randint(key_full, (), 0, N_SEQ, jnp.int32)
    slot_score = noise_score + (shard_level[slot_shard] * 2 ** 14)[None, :]
    slot_score = slot_score + jnp.where(slot_shard == full_shard, 2 ** 20, 0)[None, :]
    slot_score = slot_score * slot_count + slot_ids[None, :]
    chosen = lax.top_k(slot_score, request_count)[1].astype(jnp.int32)
    order_score = jax.random.randint(key_order, (N_SEQ, request_count), 0, 2 ** 16, jnp.int32) * request_count
    order_score = order_score + jnp.arange(request_count, dtype=jnp.int32)[None, :]
    chosen = jnp.take_along_axis(chosen, jnp.argsort(order_score, axis=1), axis=1)
    offset_score = jax.random.randint(key_offset, (N_SEQ, N_SEQ, BLOCKS_DEV), 0, 2 ** 16, jnp.int32) * BLOCKS_DEV
    offset_score = offset_score + jnp.arange(BLOCKS_DEV, dtype=jnp.int32)
    offset_table = jnp.argsort(offset_score, axis=2).astype(jnp.int32).reshape(N_SEQ, N_SEQ * BLOCKS_DEV)
    chosen_shard = chosen // CAP
    chosen_rank = chosen % CAP
    chosen_offset = jnp.take_along_axis(offset_table, chosen_shard * BLOCKS_DEV + chosen_rank, axis=1)
    return (chosen_shard * BLOCKS_DEV + chosen_offset).reshape(WINDOWS, K).astype(jnp.int32)


def levels(own_key, shape, pieces, least, top_value):
    loudness = 1.0
    for position, shards_of in pieces:
        steps = jax.random.uniform(jax.random.fold_in(jax.random.fold_in(own_key, 6), position), (shards_of,), jnp.float32, least / len(pieces), top_value / len(pieces))
        loudness = loudness * jnp.repeat(jnp.exp(steps), shape[position] // shards_of).reshape((-1,) + (1,) * (len(shape) - 1 - position))
    return loudness


def normal_values(key, shape, scale, most, pieces=(), held_as=jnp.bfloat16):
    level = levels(key, shape, pieces, -0.22, 0.18) if pieces else 1.0
    values = jax.random.normal(key, shape, jnp.float32) * scale * level
    return jnp.minimum(jnp.maximum(values, -most), most).astype(held_as)


def setup_inputs(seed: int = 0, part: int = 0) -> dict:
    key_list = jax.random.split(jax.random.key(seed), 9)
    part_splits = jax.random.split(jax.random.fold_in(key_list[8], part), 9)
    queries = draw_queries(jax.random.fold_in(jax.random.fold_in(key_list[8], part), 71), part)
    database = draw_database(jax.random.fold_in(key_list[8], 71), part)
    nbr_ids = draw_nbr_ids(jax.random.fold_in(jax.random.fold_in(key_list[8], part), 71), part)
    norm_gain = jnp.clip(1.0 + 0.15 * jax.random.normal(key_list[3], (DE,), jnp.float32), 0.25, 1.75).astype(jnp.bfloat16)
    enc_qkv = draw_enc_qkv(jax.random.fold_in(key_list[8], 71), part)
    enc_out = normal_values(key_list[5], (DE, DE), (DE // 16) ** -0.5, 0.75, ((0, 4),))
    out_gain = jnp.clip(1.0 + 0.15 * jax.random.normal(key_list[6], (DE,), jnp.float32), 0.25, 1.75).astype(jnp.bfloat16)
    cca_kv = normal_values(key_list[7], (2, DE, QW), DE ** -0.5, 0.1875, ((2, 4),))
    return dict(queries=queries, database=database, nbr_ids=nbr_ids, norm_gain=norm_gain, enc_qkv=enc_qkv, enc_out=enc_out, out_gain=out_gain, cca_kv=cca_kv)


EPSILON = 1e-06

def rounded(values):
    return lax.optimization_barrier(values.astype(jnp.bfloat16))

def rms_scale(values, scale_gain):
    wide_values = values.astype(jnp.float32)
    mean_sq = lax.optimization_barrier(jnp.mean(wide_values * wide_values, axis=-1, keepdims=True))
    return wide_values * lax.rsqrt(mean_sq + EPSILON) * scale_gain.astype(jnp.float32)

def head_mix(query_rows, key_rows, value_rows, head_size):
    leading, row_count, width_all = query_rows.shape
    key_count = key_rows.shape[1]
    head_count = width_all // head_size
    query_heads = query_rows.astype(jnp.float32).reshape(leading, row_count, head_count, head_size)
    key_heads = key_rows.astype(jnp.float32).reshape(leading, key_count, head_count, head_size)
    value_heads = value_rows.astype(jnp.float32).reshape(leading, key_count, head_count, head_size)
    scores = jnp.einsum('aqhc,akhc->ahqk', query_heads, key_heads) / math.sqrt(head_size)
    attn_probs = rounded(jax.nn.softmax(scores, axis=-1)).astype(jnp.float32)
    mixed = jnp.einsum('ahqk,akhc->aqhc', attn_probs, value_heads)
    return mixed.reshape(leading, row_count, width_all)

def reference(queries, database, nbr_ids, norm_gain, enc_qkv, enc_out, out_gain, cca_kv):
    qkv_wide = enc_qkv.astype(jnp.float32)
    out_wide = enc_out.astype(jnp.float32).reshape(N_TENSOR, DE // N_TENSOR, DE)
    cross_wide = cca_kv.astype(jnp.float32)
    padded = jnp.concatenate([jnp.zeros((1, QW), jnp.bfloat16), queries, jnp.zeros((M - 1, QW), jnp.bfloat16)], axis=0)
    groups = padded.reshape(WINDOWS + 1, M, QW)[1:]

    def one_window(payload):
        block_ids, query_group = payload
        neighbours = jnp.take(database, block_ids, axis=0)
        normed = rounded(rms_scale(neighbours, norm_gain))
        projected = rounded(jnp.einsum('nrd,jde->jnre', normed.astype(jnp.float32), qkv_wide))
        context = rounded(head_mix(projected[0], projected[1], projected[2], HDE))
        by_group = context.astype(jnp.float32).reshape(K, R, N_TENSOR, DE // N_TENSOR)
        partial_value = rounded(jnp.einsum('nrgc,gcd->nrgd', by_group, out_wide))
        update = lax.optimization_barrier(jnp.sum(partial_value.astype(jnp.float32), axis=2))
        encoded = rounded(rms_scale(neighbours.astype(jnp.float32) + update, out_gain))
        pair_rows = rounded(jnp.einsum('nrd,jde->jnre', encoded.astype(jnp.float32), cross_wide))
        pair_rows = pair_rows.reshape(2, 1, K * R, QW)
        return rounded(head_mix(query_group[None], pair_rows[0], pair_rows[1], HD))[0]
    results = lax.map(one_window, (nbr_ids, groups))
    padded_out = jnp.concatenate([jnp.zeros((M, QW), jnp.bfloat16), results.reshape(WINDOWS * M, QW)], axis=0)
    return padded_out[1:TOKENS + 1]
```

```python
import functools

import jax
import jax.numpy as jnp
from jax import lax
from jax.experimental import pallas as pl
from jax.experimental.pallas import tpu as pltpu
from jax.sharding import PartitionSpec as P

NZ, NX, NY, NC = 8, 4, 4, 2
BLOCKS = 16
ROWS = 128
PART = 16
D = 1024
SLOTS = 16
M = 64
EPS = 1e-6
CHUNKS = (256, 256, 256, 128, 128)
STARTS = tuple(sum(CHUNKS[:i]) for i in range(len(CHUNKS)))
NF = len(CHUNKS)
BF = jnp.bfloat16
F32 = jnp.float32


def body(
    ids_in, queries, database, norm_gain, enc_qkv, enc_out, out_gain, cca_kv,
    out,
    *scratch,
):
    scratch = list(scratch)

    def take(n):
        got = scratch[:n]
        del scratch[:n]
        return got

    pool, s1, r1, s2, r2, fin = (take(NF) for _ in range(6))
    (
        idv, ids_s, nb, wqkv, wout, wcca, enc, qraw, halo, qpad, back_out, back_in,
        normed, ctx, upd,
        id_sem, load_sem, z_send, z_recv, x_send, x_recv, a_send, a_recv, a_own,
        w_send, w_recv, b_send, b_recv, e_send, e_recv, h_send, h_recv,
    ) = scratch

    seq = lax.axis_index("seq")
    y = lax.axis_index("tensor")
    c = lax.axis_index("dp")
    z = seq // NX
    x = lax.rem(seq, NX)
    part = 2 * y + c

    def at(dz=0, dx=0, dy=0, dc=0):
        return {
            "seq": lax.rem(z + dz + NZ, NZ) * NX + lax.rem(x + dx + NX, NX),
            "tensor": lax.rem(y + dy + NY, NY),
            "dp": lax.rem(c + dc, NC),
        }

    def along(ds):
        return {"seq": lax.rem(seq + ds + NZ * NX, NZ * NX), "tensor": y, "dp": c}

    started = []

    def remote(src, dst, send_sem, recv_sem, device):
        return pltpu.make_async_remote_copy(
            src_ref=src, dst_ref=dst, send_sem=send_sem, recv_sem=recv_sem,
            device_id=device, device_id_type=pl.DeviceIdType.MESH,
        )

    def go(copy):
        copy.start()
        started.append(copy)

    def own_piece(f):
        return pltpu.make_async_copy(
            database.at[:, pl.ds(pl.multiple_of(PART * part, PART), PART), pl.ds(STARTS[f], CHUNKS[f])],
            pool[f].at[pl.ds(0, BLOCKS)], load_sem.at[f],
        )

    for f in range(NF):
        own_piece(f).start()
    ycol = pl.ds(pl.multiple_of(256 * y, 256), 256)
    local = [
        pltpu.make_async_copy(enc_qkv, wqkv.at[:, :, ycol], load_sem.at[NF]),
        pltpu.make_async_copy(enc_out, wout.at[ycol], load_sem.at[NF + 1]),
        pltpu.make_async_copy(cca_kv, wcca, load_sem.at[NF + 2]),
        pltpu.make_async_copy(queries, qraw, load_sem.at[NF + 3]),
    ]
    for copy in local:
        copy.start()
    idv[0] = jnp.zeros((8, 128), jnp.int32)
    idv[0, :, 0:2] = ids_in[...]

    greet = [at(dz=1), at(dz=-1), along(1), along(-1)]
    greet += [at(dx=dx, dc=dc) for dx in range(NX) for dc in range(NC) if dx or dc]
    greet += [at(dy=dy, dc=dc) for dy in range(1, NY) for dc in range(NC)]
    barrier = pltpu.get_barrier_semaphore()
    for device in greet:
        pl.semaphore_signal(barrier, inc=1, device_id=device, device_id_type=pl.DeviceIdType.MESH)
    pl.semaphore_wait(barrier, len(greet))

    def z_copy(f, right, k):
        count = BLOCKS if k < 4 else BLOCKS // 2
        shift = 0 if (k < 4 or right) else BLOCKS // 2
        source = (k - 1) if right else (NZ - (k - 1)) % NZ
        target = k if right else NZ - k
        i = (k - 1) if right else 4 + (k - 1)
        return remote(
            pool[f].at[pl.ds(BLOCKS * source + shift, count)],
            pool[f].at[pl.ds(BLOCKS * target + shift, count)],
            z_send.at[f, i], z_recv.at[f, i], at(dz=1 if right else -1),
        )

    def id_copy(dx, dc):
        slot = ((NX - dx) % NX) * 2 + dc
        return remote(idv.at[0], idv.at[slot], id_sem.at[slot], id_sem.at[8 + slot], at(dx=dx, dc=dc))

    def x_first(f, half):
        return remote(
            s1[f].at[half], r1[f].at[half], x_send.at[f, half], x_recv.at[f, half],
            at(dx=-1 if half == 0 else 1),
        )

    def x_second(f, right, half):
        i = 2 + 2 * right + half
        return remote(
            s2[f].at[right, half], r2[f].at[right, half], x_send.at[f, i], x_recv.at[f, i],
            at(dx=1 if right else -1),
        )

    def rows_of(f):
        return (slice(None), pl.ds(pl.multiple_of(PART * part, PART), PART), pl.ds(STARTS[f], CHUNKS[f]))

    def a_copy(f, dy, dc):
        t = lax.rem(y + dy, NY)
        i = dy * 2 + dc
        return remote(
            fin[f].at[dc, pl.ds(4 * t, 4)], nb.at[rows_of(f)],
            a_send.at[f, i], a_recv.at[f, i], at(dy=dy, dc=dc),
        )

    def a_local(f):
        return pltpu.make_async_copy(fin[f].at[0, pl.ds(4 * y, 4)], nb.at[rows_of(f)], a_own.at[f])

    def w_place(unit, rel, of=None):
        t = lax.rem(y + rel + NY, NY)
        if unit < 3:
            return wqkv.at[unit, pl.ds(pl.multiple_of(512 * c, 512), 512), pl.ds(pl.multiple_of(256 * t, 256), 256)]
        return wout.at[pl.ds(pl.multiple_of(256 * t + 128 * c, 128), 128)]

    def w_own(unit):
        if unit < 3:
            return enc_qkv.at[unit, pl.ds(pl.multiple_of(512 * c, 512), 512)]
        return enc_out.at[pl.ds(pl.multiple_of(128 * c, 128), 128)]

    def w_first(unit, right):
        i = unit + 4 * right
        return remote(w_own(unit), w_place(unit, 0), w_send.at[i], w_recv.at[i], at(dy=1 if right else -1))

    def w_second(unit):
        right = unit < 2
        return remote(
            w_place(unit, -1 if right else 1), w_place(unit, -1 if right else 1),
            w_send.at[8 + unit], w_recv.at[8 + unit], at(dy=1 if right else -1),
        )

    def w_twin(unit, rel):
        i = unit + 4 * (rel - 1)
        return remote(w_place(unit, rel), w_place(unit, rel), b_send.at[i], b_recv.at[i], at(dc=1))

    def e_place(late, n, rel):
        t = lax.rem(y + rel + NY, NY)
        return enc.at[2 * t + late, pl.ds(ROWS * n, ROWS)]

    def e_first(late, n, right):
        i = late * 6 + n * 2 + right
        return remote(
            e_place(late, n, 0), e_place(late, n, 0), e_send.at[i], e_recv.at[i], at(dy=1 if right else -1)
        )

    def e_second(late, n):
        i = late * 6 + 4 + n
        rel = -1 if n == 0 else 1
        return remote(
            e_place(late, n, rel), e_place(late, n, rel), e_send.at[i], e_recv.at[i], at(dy=-rel)
        )

    def h_query():
        return remote(queries.at[pl.ds(0, M)], halo, h_send.at[0], h_recv.at[0], along(-1))

    def h_back():
        return remote(back_out, back_in, h_send.at[1], h_recv.at[1], along(1))

    def select(f, requester, core, j, other):
        b = ids_s[2 * requester + core, j // 2, lax.rem(j, 2)]
        index = lax.rem(z - b // (NX * BLOCKS) + NZ, NZ) * BLOCKS + lax.rem(b, BLOCKS)
        owner = lax.rem(b // BLOCKS, NX)
        mine = pool[f][index]
        return mine if other is None else other(mine, owner)

    def first_select(f):
        def step(i, carry):
            core, j = i // 8, lax.rem(i, 8)
            s1[f][0, core, j] = select(f, 2, core, j, None)
            s1[f][1, core, j] = select(f, 2, core, 8 + j, None)
            return carry

        lax.fori_loop(0, 16, step, 0, unroll=2)

    def plain_select(f):
        def step(i, carry):
            core, j = i // 8, lax.rem(i, 8)
            s2[f][0, 1, core, j] = select(f, 3, core, 8 + j, None)
            s2[f][1, 0, core, j] = select(f, 1, core, j, None)
            return carry

        lax.fori_loop(0, 16, step, 0, unroll=2)

    def merge_select(f):
        def step(i, carry):
            core, j = i // 8, lax.rem(i, 8)
            s2[f][0, 0, core, j] = select(
                f, 3, core, j, lambda mine, owner: jnp.where(owner == x, mine, r1[f][0, core, j])
            )
            s2[f][1, 1, core, j] = select(
                f, 1, core, 8 + j, lambda mine, owner: jnp.where(owner == x, mine, r1[f][1, core, j])
            )
            return carry

        lax.fori_loop(0, 16, step, 0, unroll=2)

    def last_select(f):
        left, right = lax.rem(x + NX - 1, NX), lax.rem(x + 1, NX)

        def step(i, carry):
            core, j = i // 8, lax.rem(i, 8)

            def half0(mine, owner):
                far = jnp.where(owner == left, r2[f][1, 0, core, j], r2[f][0, 0, core, j])
                return jnp.where(owner == x, mine, far)

            def half1(mine, owner):
                far = jnp.where(owner == right, r2[f][0, 1, core, j], r2[f][1, 1, core, j])
                return jnp.where(owner == x, mine, far)

            fin[f][core, j] = select(f, 0, core, j, half0)
            fin[f][core, 8 + j] = select(f, 0, core, 8 + j, half1)
            return carry

        lax.fori_loop(0, 16, step, 0, unroll=2)

    def shift_queries():
        top = lax.broadcasted_iota(jnp.int32, (M, D), 0) == 0
        before = jnp.zeros((M, D), F32)
        for g in range(9):
            tile = qraw[pl.ds(M * g, M)] if g < 8 else halo[...]
            turned = pltpu.roll(tile.astype(F32), 1, 0)
            qpad[g] = jnp.where(top, before, turned).astype(BF)
            before = turned

    def encode(late):
        blocks = pl.ds(2 * late, 2)
        raw = nb[blocks].reshape(2 * ROWS, D).astype(F32)
        scale = lax.rsqrt(jnp.mean(raw * raw, axis=1, keepdims=True) + EPS)
        normed[...] = (raw * scale * norm_gain[...].astype(F32)).astype(BF)
        low = lax.broadcasted_iota(jnp.int32, (ROWS, 128), 1) < 64
        zero = jnp.zeros((ROWS, 128), BF)

        def heads(g, carry):
            cols = pl.ds(pl.multiple_of(256 * g, 256), 256)
            rows = normed[...]
            q, k, v = (
                jnp.dot(rows, wqkv[j, :, cols], preferred_element_type=F32).astype(BF) for j in range(3)
            )
            mixed = []
            for n in range(2):
                pairs = []
                for p in range(2):
                    cut = (slice(ROWS * n, ROWS * (n + 1)), slice(128 * p, 128 * (p + 1)))
                    qp, kp, vp = q[cut], k[cut], v[cut]
                    k2 = jnp.concatenate([jnp.where(low, kp, zero), jnp.where(low, zero, kp)], axis=0)
                    v2 = jnp.concatenate([jnp.where(low, vp, zero), jnp.where(low, zero, vp)], axis=0)
                    s = lax.dot_general(qp, k2, (((1,), (1,)), ((), ())), preferred_element_type=F32) * 0.125
                    probs = []
                    for h in range(2):
                        sh = s[:, 128 * h : 128 * (h + 1)]
                        e = jnp.exp(sh - jnp.max(sh, axis=1, keepdims=True))
                        probs.append((e / jnp.sum(e, axis=1, keepdims=True)).astype(BF))
                    pairs.append(jnp.dot(jnp.concatenate(probs, axis=1), v2, preferred_element_type=F32).astype(BF))
                mixed.append(jnp.concatenate(pairs, axis=1))
            ctx[:, cols] = jnp.concatenate(mixed, axis=0)
            return carry

        lax.fori_loop(0, 4, heads, 0)

        def project(g, carry):
            cols = pl.ds(pl.multiple_of(256 * g, 256), 256)
            upd[:, cols] = jnp.dot(ctx[...], wout[:, cols], preferred_element_type=F32)
            return carry

        lax.fori_loop(0, 4, project, 0)
        total = upd[...] + nb[blocks].reshape(2 * ROWS, D).astype(F32)
        scale = lax.rsqrt(jnp.mean(total * total, axis=1, keepdims=True) + EPS)
        enc[2 * y + late] = (total * scale * out_gain[...].astype(F32)).astype(BF)

    def attend(rel, late):
        w = 2 * lax.rem(y + rel + NY, NY) + late

        def heads(g, carry):
            cols = pl.ds(pl.multiple_of(256 * g, 256), 256)
            rows = enc[w]
            k = jnp.dot(rows, wcca[0, :, cols], preferred_element_type=F32).astype(BF)
            v = jnp.dot(rows, wcca[1, :, cols], preferred_element_type=F32).astype(BF)
            q = qpad[w + 1, :, cols]
            mixed = []
            for h in range(2):
                cut = slice(128 * h, 128 * (h + 1))
                s = lax.dot_general(
                    q[:, cut], k[:, cut], (((1,), (1,)), ((), ())), preferred_element_type=F32
                ) * (128.0 ** -0.5)
                e = jnp.exp(s - jnp.max(s, axis=1, keepdims=True))
                p = (e / jnp.sum(e, axis=1, keepdims=True)).astype(BF)
                mixed.append(jnp.dot(p, v[:, cut], preferred_element_type=F32).astype(BF))
            out[w + 1, :, cols] = jnp.concatenate(mixed, axis=1)
            return carry

        lax.fori_loop(0, 4, heads, 0)

    def z_step(f, k):
        if k == 1:
            own_piece(f).wait()
        else:
            z_copy(f, True, k - 1).wait_recv()
            z_copy(f, False, k - 1).wait_recv()
        go(z_copy(f, True, k))
        go(z_copy(f, False, k))

    def x_step1(f):
        z_copy(f, True, 4).wait_recv()
        z_copy(f, False, 4).wait_recv()
        first_select(f)
        go(x_first(f, 0))
        go(x_first(f, 1))
        plain_select(f)
        go(x_second(f, 0, 1))
        go(x_second(f, 1, 0))

    def x_step2(f):
        x_first(f, 0).wait_recv()
        x_first(f, 1).wait_recv()
        merge_select(f)
        go(x_second(f, 0, 0))
        go(x_second(f, 1, 1))

    others = [(dy, dc) for dy in (2, 1, 3, 0) for dc in range(NC) if dy or dc]

    def x_step3(f):
        for right in range(2):
            for half in range(2):
                x_second(f, right, half).wait_recv()
        last_select(f)
        for dy, dc in others:
            go(a_copy(f, dy, dc))
        a_local(f).start()

    def w_forward(pos):
        for right in (1, 0):
            unit = pos if right else (pos + 2) % 4
            w_first(unit, right).wait_recv()
            if pos < 2:
                go(w_second(unit))
            go(w_twin(unit, 3 if right else 1))

    for f in range(2):
        z_step(f, 1)
    for dx in range(NX):
        for dc in range(NC):
            if dx or dc:
                go(id_copy(dx, dc))
    go(h_query())
    for pos in range(4):
        go(w_first(pos, 1))
        go(w_first((pos + 2) % 4, 0))

    events = []
    for f in range(NF):
        for k in range(1, 5):
            if k > 1 or f > 1:
                events.append((2 * f + k, 0, functools.partial(z_step, f, k)))
        events.append((2 * f + 5, 2, functools.partial(x_step1, f)))
        events.append((2 * f + 6, 3, functools.partial(x_step2, f)))
        events.append((2 * f + 7, 4, functools.partial(x_step3, f)))

    def ids_ready():
        for dx in range(NX):
            for dc in range(NC):
                if dx or dc:
                    id_copy(dx, dc).wait_recv()
        copy = pltpu.make_async_copy(idv, ids_s, id_sem.at[0])
        copy.start()
        copy.wait()

    def queries_ready():
        local[3].wait()
        h_query().wait_recv()
        shift_queries()

    events.append((3, 1, ids_ready))
    events.append((4, 1, queries_ready))
    for pos, tick in enumerate((4, 6, 8, 10)):
        events.append((tick, 5, functools.partial(w_forward, pos)))
    events.sort(key=lambda e: e[:2])
    for _, _, event in events:
        event()

    for unit in range(4):
        w_second(unit).wait_recv()
        go(w_twin(unit, 2))
    for f in range(NF):
        for dy, dc in others:
            a_copy(f, dy, dc).wait_recv()
        a_local(f).wait()
    for rel in range(1, 4):
        for unit in range(4):
            w_twin(unit, rel).wait_recv()
    for i in range(3):
        local[i].wait()

    def e_forward(late):
        for n in range(2):
            rel_right = n == 0
            e_first(late, n, 1 if rel_right else 0).wait_recv()
            go(e_second(late, n))

    for late in (1, 0):
        encode(late)
        go(e_first(late, 0, 1))
        go(e_first(late, 1, 0))
        go(e_first(late, 1, 1))
        go(e_first(late, 0, 0))
    e_forward(1)
    attend(0, 1)
    attend(0, 0)
    e_first(1, 1, 1).wait_recv()
    attend(-1, 1)
    e_first(1, 0, 0).wait_recv()
    attend(1, 1)
    e_forward(0)
    e_first(0, 1, 1).wait_recv()
    attend(-1, 0)
    e_first(0, 0, 0).wait_recv()
    attend(1, 0)
    for n in range(2):
        e_second(1, n).wait_recv()
    attend(2, 1)
    back_out[...] = out[8]
    go(h_back())
    for n in range(2):
        e_second(0, n).wait_recv()
    attend(2, 0)
    h_back().wait_recv()
    out[0] = back_in[...]
    for copy in started:
        copy.wait_send()


def fused(ids, queries, database, norm_gain, enc_qkv, enc_out, out_gain, cca_kv):
    dma = pltpu.SemaphoreType.DMA
    per_chunk = lambda *lead: [pltpu.VMEM(lead + (PART, w), BF) for w in CHUNKS]
    scratch = (
        per_chunk(NZ * BLOCKS)
        + per_chunk(2, 2, 8) + per_chunk(2, 2, 8)
        + per_chunk(2, 2, 2, 8) + per_chunk(2, 2, 2, 8)
        + per_chunk(2, SLOTS)
    )
    scratch += [
        pltpu.VMEM((8, 8, 128), jnp.int32),
        pltpu.SMEM((8, 8, 128), jnp.int32),
        pltpu.VMEM((4, ROWS, D), BF),
        pltpu.VMEM((3, D, D), BF),
        pltpu.VMEM((D, D), BF),
        pltpu.VMEM((2, D, D), BF),
        pltpu.VMEM((8, 2 * ROWS, D), BF),
        pltpu.VMEM((8 * M, D), BF),
        pltpu.VMEM((M, D), BF),
        pltpu.VMEM((9, M, D), BF),
        pltpu.VMEM((M, D), BF),
        pltpu.VMEM((M, D), BF),
        pltpu.VMEM((2 * ROWS, D), BF),
        pltpu.VMEM((2 * ROWS, D), BF),
        pltpu.VMEM((2 * ROWS, D), F32),
        dma((16,)), dma((NF + 4,)), dma((NF, 8)), dma((NF, 8)), dma((NF, 6)), dma((NF, 6)),
        dma((NF, 8)), dma((NF, 8)), dma((NF,)),
        dma((12,)), dma((12,)), dma((12,)), dma((12,)), dma((12,)), dma((12,)), dma((2,)), dma((2,)),
    ]
    vmem = pl.BlockSpec(memory_space=pltpu.VMEM)
    hbm = pl.BlockSpec(memory_space=pl.ANY)
    return pl.pallas_call(
        body,
        out_shape=jax.ShapeDtypeStruct((9, M, D), BF),
        in_specs=[vmem, hbm, hbm, vmem, hbm, hbm, vmem, hbm],
        out_specs=vmem,
        scratch_shapes=scratch,
        compiler_params=pltpu.CompilerParams(
            collective_id=0, has_side_effects=True, vmem_limit_bytes=56 * 2**20
        ),
        cost_estimate=pl.CostEstimate(flops=14 * 10**9, bytes_accessed=12 * 2**20, transcendentals=4 * 10**6),
    )(ids, queries, database, norm_gain, enc_qkv, enc_out, out_gain, cca_kv)


def per_device(queries, database, nbr_ids, norm_gain, enc_qkv, enc_out, out_gain, cca_kv):
    groups = fused(
        nbr_ids, queries, database, norm_gain.reshape(1, D), enc_qkv, enc_out, out_gain.reshape(1, D), cca_kv
    )
    tokens = queries.shape[0]
    attended = groups.reshape(9 * M, D)[1 : tokens + 1]
    unserved = (lax.axis_index("seq") == 0) & (lax.broadcasted_iota(jnp.int32, (tokens, 1), 0) < M - 1)
    return jnp.where(unserved, jnp.zeros((), BF), attended)


def solution(mesh):
    placed = (
        P(("dp", "seq"), "tensor"),
        P("seq", None, None),
        P(("dp", "seq"), None),
        P(),
        P(None, None, "tensor"),
        P("tensor", None),
        P(),
        P(None, None, "tensor"),
    )
    return jax.shard_map(
        per_device,
        mesh=mesh,
        in_specs=placed,
        out_specs=P(("dp", "seq"), "tensor"),
        check_vma=False,
    )
```

```python
import functools

import jax
import jax.numpy as jnp
from jax import lax
from jax.experimental import pallas as pl
from jax.experimental.pallas import tpu as pltpu
from jax.sharding import PartitionSpec as P

NZ, NX, NY, NC = 8, 4, 4, 2
BLOCKS = 16
ROWS = 128
PART = 16
D = 1024
SLOTS = 16
M = 64
EPS = 1e-6
NF = 8
WIDE = D // NF
UNITS = ((1, (0, 1)), (1, (2, 3)), (1, (4, 5)), (1, (6,)), (1, (7,)), (0, (0, 1, 2, 3)), (0, (4, 5, 6, 7)))
DIRECT = ()
SHARED = 12
EACH = SHARED // NY
PLACES = tuple(3 * t + (m if t % 2 == 0 else 2 - m) for t in range(NY) for m in range(EACH)) + (12, 13, 14, 15)
ORDER = (
    ('z', 2, 1), ('z', 0, 1), ('z', 1, 1), ('z', 3, 1), ('z', 0, 2), ('w0', 0),
    ('z', 1, 2), ('z', 2, 2), ('z', 3, 2), ('w0', 1), ('z', 0, 3), ('z', 1, 3),
    ('w0', 2), ('z', 3, 3), ('ids',), ('z', 0, 4), ('z', 2, 3), ('z', 1, 4),
    ('z', 4, 1), ('zd', 0), ('z', 7, 1), ('z', 2, 4), ('z', 3, 4), ('z', 5, 1),
    ('zd', 1), ('x1', 0), ('z', 4, 2), ('wf', 0), ('z', 7, 2), ('zd', 2),
    ('zd', 3), ('x1', 1), ('z', 6, 1), ('x2', 0), ('z', 5, 2), ('wf', 1),
    ('z', 7, 3), ('x1', 5), ('z', 4, 3), ('z', 5, 3), ('x2', 1), ('z', 7, 4),
    ('w0', 3), ('z', 6, 2), ('x3', 0), ('z', 4, 4), ('x2', 5), ('z', 5, 4),
    ('wr', 0), ('zd', 7), ('x1', 4), ('z', 6, 3), ('zd', 4), ('zd', 5),
    ('x1', 2), ('wr', 1), ('z', 6, 4), ('x3', 1), ('x2', 4), ('x2', 2),
    ('zd', 6), ('x1', 3), ('wf', 2), ('x3', 5), ('x1', 6), ('q',),
    ('x2', 3), ('x3', 2), ('x2', 6), ('x3', 4), ('wf', 3), ('x3', 3),
    ('x3', 6), ('en', 0), ('en', 1), ('en', 2), ('en', 3), ('er', 0, 0),
    ('er', 0, 1), ('er', 0, 2), ('ef', 0), ('er', 1, 0), ('er', 1, 1), ('er', 1, 2),
    ('at', 6), ('ef', 1), ('at', 7), ('hb',), ('at', 0), ('ar',),
    ('at', 1), ('ef', 2), ('at', 2), ('at', 3), ('at', 4), ('at', 5),
)
LOG2E = 1.4426950408889634
BF = jnp.bfloat16
F32 = jnp.float32


def body(
    ids_in, queries, database, norm_gain, enc_qkv, enc_out, out_gain, cca_kv,
    out,
    *scratch,
):
    scratch = list(scratch)

    def take(n):
        got = scratch[:n]
        del scratch[:n]
        return got

    pool = take(NF)
    s1, r1, s2, r2, fin = (take(len(UNITS)) for _ in range(5))
    (
        idv, ids_s, table, nbp, nbr, wqkv, wout, wcca, enc, qraw, halo, qpad, back_out, back_in,
        normed, ctx, upd, qs, kv,
        id_sem, load_sem, z_send, z_recv, x_send, x_recv, a_send, a_recv, a_own,
        w_send, w_recv, b_send, b_recv, e_send, e_recv, h_send, h_recv,
    ) = scratch

    seq = lax.axis_index("seq")
    y = lax.axis_index("tensor")
    c = lax.axis_index("dp")
    z = seq // NX
    x = lax.rem(seq, NX)
    part = 2 * y + c

    def at(dz=0, dx=0, dy=0, dc=0):
        return {
            "seq": lax.rem(z + dz + NZ, NZ) * NX + lax.rem(x + dx + NX, NX),
            "tensor": lax.rem(y + dy + NY, NY),
            "dp": lax.rem(c + dc, NC),
        }

    def along(ds):
        return {"seq": lax.rem(seq + ds + NZ * NX, NZ * NX), "tensor": y, "dp": c}

    started = []

    def remote(src, dst, send_sem, recv_sem, device):
        return pltpu.make_async_remote_copy(
            src_ref=src, dst_ref=dst, send_sem=send_sem, recv_sem=recv_sem,
            device_id=device, device_id_type=pl.DeviceIdType.MESH,
        )

    def go(copy):
        copy.start()
        started.append(copy)

    def own_piece(f):
        return pltpu.make_async_copy(
            database.at[:, pl.ds(pl.multiple_of(PART * part, PART), PART), pl.ds(WIDE * f, WIDE)],
            pool[f].at[pl.ds(0, BLOCKS)], load_sem.at[f],
        )

    for f in range(NF):
        own_piece(f).start()
    ycol = pl.ds(pl.multiple_of(256 * y, 256), 256)
    local = [
        pltpu.make_async_copy(enc_qkv, wqkv.at[:, :, ycol], load_sem.at[NF]),
        pltpu.make_async_copy(enc_out, wout.at[ycol], load_sem.at[NF + 1]),
        pltpu.make_async_copy(cca_kv, wcca, load_sem.at[NF + 2]),
        pltpu.make_async_copy(queries, qraw, load_sem.at[NF + 3]),
    ]
    for copy in local:
        copy.start()
    idv[0] = jnp.zeros((8, 128), jnp.int32)
    idv[0, 0:2, 0:8] = ids_in[...]

    greet = [at(dz=1), at(dz=-1), along(1), along(-1)]
    greet += [at(dx=dx, dc=dc) for dx in range(NX) for dc in range(NC) if dx or dc]
    greet += [at(dy=dy, dc=dc) for dy in range(1, NY) for dc in range(NC)]
    barrier = pltpu.get_barrier_semaphore()
    for device in greet:
        pl.semaphore_signal(barrier, inc=1, device_id=device, device_id_type=pl.DeviceIdType.MESH)
    pl.semaphore_wait(barrier, len(greet))

    def z_copy(f, right, k):
        count = BLOCKS if k < 4 else BLOCKS // 2
        shift = 0 if (k < 4 or right) else BLOCKS // 2
        source = (k - 1) if right else (NZ - (k - 1)) % NZ
        target = k if right else NZ - k
        i = (k - 1) if right else 4 + (k - 1)
        return remote(
            pool[f].at[pl.ds(BLOCKS * source + shift, count)],
            pool[f].at[pl.ds(BLOCKS * target + shift, count)],
            z_send.at[f, i], z_recv.at[f, i], at(dz=1 if right else -1),
        )

    def id_copy(dx, dc):
        slot = ((NX - dx) % NX) * 2 + dc
        return remote(idv.at[0], idv.at[slot], id_sem.at[slot], id_sem.at[8 + slot], at(dx=dx, dc=dc))

    def x_first(u, half):
        return remote(
            s1[u].at[half], r1[u].at[half], x_send.at[u, half], x_recv.at[u, half],
            at(dx=2 if u in DIRECT else -1 if half == 0 else 1),
        )

    def x_second(u, right, half):
        i = 2 + 2 * right + half
        return remote(
            s2[u].at[right, half], r2[u].at[right, half], x_send.at[u, i], x_recv.at[u, i],
            at(dx=1 if right else -1),
        )

    def a_ends(u, core, t):
        shared, chunks = UNITS[u]
        where = (
            slice(None), pl.ds(pl.multiple_of(PART * part, PART), PART),
            pl.ds(WIDE * chunks[0], WIDE * len(chunks)),
        )
        if shared:
            return fin[u].at[core, pl.ds(EACH * t, EACH)], nbp.at[where]
        return fin[u].at[core], nbr.at[where]

    def a_copy(u, dy, dc):
        i = dy * 2 + dc
        return remote(*a_ends(u, dc, lax.rem(y + dy, NY)), a_send.at[u, i], a_recv.at[u, i], at(dy=dy, dc=dc))

    def a_local(u):
        return pltpu.make_async_copy(*a_ends(u, 0, y), a_own.at[u])

    def w_place(unit, rel, of=None):
        t = lax.rem(y + rel + NY, NY)
        if unit < 3:
            return wqkv.at[unit, pl.ds(pl.multiple_of(512 * c, 512), 512), pl.ds(pl.multiple_of(256 * t, 256), 256)]
        return wout.at[pl.ds(pl.multiple_of(256 * t + 128 * c, 128), 128)]

    def w_own(unit):
        if unit < 3:
            return enc_qkv.at[unit, pl.ds(pl.multiple_of(512 * c, 512), 512)]
        return enc_out.at[pl.ds(pl.multiple_of(128 * c, 128), 128)]

    def w_first(unit, right):
        i = unit + 4 * right
        return remote(w_own(unit), w_place(unit, 0), w_send.at[i], w_recv.at[i], at(dy=1 if right else -1))

    def w_second(unit):
        right = unit < 2
        return remote(
            w_place(unit, -1 if right else 1), w_place(unit, -1 if right else 1),
            w_send.at[8 + unit], w_recv.at[8 + unit], at(dy=1 if right else -1),
        )

    def w_twin(unit, rel):
        i = unit + 4 * (rel - 1)
        return remote(w_place(unit, rel), w_place(unit, rel), b_send.at[i], b_recv.at[i], at(dc=1))

    def e_slot(m, rel):
        t = lax.rem(y + rel + NY, NY)
        return 3 * t + m + lax.rem(t, 2) * (2 - 2 * m)

    def e_first(m, right):
        i = 2 * m + right
        place = enc.at[e_slot(m, 0)]
        return remote(place, place, e_send.at[i], e_recv.at[i], at(dy=1 if right else -1))

    def e_second(m, right):
        i = 6 + m + (1 if m == 2 and not right else 0)
        rows = pl.ds(0, ROWS) if m < 2 else pl.ds(0 if right else ROWS // 2, ROWS // 2)
        place = enc.at[e_slot(m, -1 if right else 1), rows]
        return remote(place, place, e_send.at[i], e_recv.at[i], at(dy=1 if right else -1))

    def h_query():
        return remote(queries.at[pl.ds(0, M)], halo, h_send.at[0], h_recv.at[0], along(-1))

    def h_back():
        return remote(back_out, back_in, h_send.at[1], h_recv.at[1], along(1))

    def fill_table():
        def step(q, carry):
            for p, j in enumerate(PLACES):
                b = ids_s[q, j % 2, j // 2]
                table[0, q, p] = ((z - (b >> 6) + NZ) & (NZ - 1)) * BLOCKS + (b & (BLOCKS - 1))
                table[1, q, p] = ((b >> 4) - x + NX) & (NX - 1)
            return carry

        lax.fori_loop(0, 8, step, 0)

    def each(u, act):
        shared, chunks = UNITS[u]
        first, count = (0, SHARED // 2) if shared else (SHARED, 2)

        def step(i, carry):
            for core in range(2):
                for n, f in enumerate(chunks):
                    act(f, core, i, (first + i, first + count + i), slice(WIDE * n, WIDE * (n + 1)))
            return carry

        lax.fori_loop(0, count, step, 0, unroll=2)

    def mine(f, requester, core, p):
        return pool[f][table[0, 2 * requester + core, p]]

    def owner(requester, core, p):
        return table[1, 2 * requester + core, p]

    def first_select(u):
        def act(f, core, i, p, cols):
            for half in range(2):
                s1[u][half, core, i, :, cols] = mine(f, 2, core, p[half])

        each(u, act)

    def plain_select(u):
        def act(f, core, i, p, cols):
            s2[u][0, 1, core, i, :, cols] = mine(f, 3, core, p[1])
            s2[u][1, 0, core, i, :, cols] = mine(f, 1, core, p[0])
            if u in DIRECT:
                s2[u][0, 0, core, i, :, cols] = mine(f, 3, core, p[0])
                s2[u][1, 1, core, i, :, cols] = mine(f, 1, core, p[1])

        each(u, act)

    def merge_select(u):
        def act(f, core, i, p, cols):
            s2[u][0, 0, core, i, :, cols] = jnp.where(
                owner(3, core, p[0]) == 0, mine(f, 3, core, p[0]), r1[u][0, core, i, :, cols]
            )
            s2[u][1, 1, core, i, :, cols] = jnp.where(
                owner(1, core, p[1]) == 0, mine(f, 1, core, p[1]), r1[u][1, core, i, :, cols]
            )

        each(u, act)

    def last_select(u):
        count = SHARED // 2 if UNITS[u][0] else 2

        def act(f, core, i, p, cols):
            for half in range(2):
                of = owner(0, core, p[half])
                right, left = r2[u][0, half, core, i, :, cols], r2[u][1, half, core, i, :, cols]
                if u in DIRECT:
                    far = jnp.where(of == 1, right, jnp.where(of == 3, left, r1[u][half, core, i, :, cols]))
                elif half == 0:
                    far = jnp.where(of == 3, left, right)
                else:
                    far = jnp.where(of == 1, right, left)
                fin[u][core, half * count + i, :, cols] = jnp.where(of == 0, mine(f, 0, core, p[half]), far)

        each(u, act)

    def shift_queries():
        top = lax.broadcasted_iota(jnp.int32, (M, D), 0) == 0
        before = jnp.zeros((M, D), F32)
        for g in range(9):
            tile = qraw[pl.ds(M * g, M)] if g < 8 else halo[...]
            turned = pltpu.roll(tile.astype(F32), 1, 0)
            qpad[g] = jnp.where(top, before, turned).astype(BF)
            before = turned

    def gain(ref):
        g = ref[...].astype(F32)
        return jnp.concatenate([g[i : i + 1] for i in range(8)], axis=1)

    def encode_in(blocks, count):
        rows = pl.ds(0, count * ROWS)
        raw = blocks[...].reshape(count * ROWS, D).astype(F32)
        scale = lax.rsqrt(jnp.mean(raw * raw, axis=1, keepdims=True) + EPS)
        normed[rows] = (raw * scale * gain(norm_gain)).astype(BF)

        def project_in(g, carry):
            cols = pl.ds(pl.multiple_of(512 * g, 512), 512)
            for j in range(3):
                qs[j, rows, cols] = jnp.dot(normed[rows], wqkv[j, :, cols], preferred_element_type=F32).astype(BF)
            return carry

        lax.fori_loop(0, 2, project_in, 0)

    def encode_mix(count):
        rows = pl.ds(0, count * ROWS)
        low = lax.broadcasted_iota(jnp.int32, (ROWS, 128), 1) < 64
        zero, one = jnp.zeros((ROWS, 128), BF), jnp.ones((ROWS, 128), BF)
        sums = jnp.concatenate([jnp.where(low, one, zero), jnp.where(low, zero, one)], axis=0)

        def heads(g, carry):
            cols = pl.ds(pl.multiple_of(256 * g, 256), 256)
            q, k, v = qs[0, rows, cols], qs[1, rows, cols], qs[2, rows, cols]
            mixed = []
            for n in range(count):
                pairs = []
                for p in range(2):
                    cut = (slice(ROWS * n, ROWS * (n + 1)), slice(128 * p, 128 * (p + 1)))
                    qp, kp, vp = q[cut], k[cut], v[cut]
                    k2 = jnp.concatenate([jnp.where(low, kp, zero), jnp.where(low, zero, kp)], axis=0)
                    v2 = jnp.concatenate([jnp.where(low, vp, zero), jnp.where(low, zero, vp)], axis=0)
                    s = lax.dot_general(qp, k2, (((1,), (1,)), ((), ())), preferred_element_type=F32)
                    probs = []
                    for h in range(2):
                        sh = s[:, 128 * h : 128 * (h + 1)]
                        top = jnp.max(sh, axis=1, keepdims=True)
                        probs.append(jnp.exp2((sh - top) * (0.125 * LOG2E)).astype(BF))
                    o = jnp.dot(
                        jnp.concatenate(probs, axis=1), jnp.concatenate([v2, sums], axis=1),
                        preferred_element_type=F32,
                    )
                    pairs.append((o[:, :128] / o[:, 128:]).astype(BF))
                mixed.append(jnp.concatenate(pairs, axis=1))
            ctx[rows, cols] = jnp.concatenate(mixed, axis=0)
            return carry

        lax.fori_loop(0, 4, heads, 0, unroll=4)

    def encode_out(blocks, count, places):
        rows = pl.ds(0, count * ROWS)

        def project_out(g, carry):
            cols = pl.ds(pl.multiple_of(512 * g, 512), 512)
            upd[rows, cols] = jnp.dot(ctx[rows], wout[:, cols], preferred_element_type=F32)
            return carry

        lax.fori_loop(0, 2, project_out, 0)
        total = upd[rows] + blocks[...].reshape(count * ROWS, D).astype(F32)
        scale = lax.rsqrt(jnp.mean(total * total, axis=1, keepdims=True) + EPS)
        done = (total * scale * gain(out_gain)).astype(BF)
        for n, place in enumerate(places):
            enc[place] = done[ROWS * n : ROWS * (n + 1)]

    def attend(w):
        rows = enc[pl.ds(2 * w, 2)].reshape(2 * ROWS, D)

        def project(g, carry):
            cols = pl.ds(pl.multiple_of(512 * g, 512), 512)
            for j in range(2):
                kv[j, :, cols] = jnp.dot(rows, wcca[j, :, cols], preferred_element_type=F32).astype(BF)
            return carry

        lax.fori_loop(0, 2, project, 0)
        count = jnp.ones((2 * ROWS, 128), BF)

        def heads(g, carry):
            cols = pl.ds(pl.multiple_of(256 * g, 256), 256)
            q, k, v = qpad[w + 1, :, cols], kv[0, :, cols], kv[1, :, cols]
            mixed = []
            for h in range(2):
                cut = slice(128 * h, 128 * (h + 1))
                s = lax.dot_general(
                    q[:, cut], k[:, cut], (((1,), (1,)), ((), ())), preferred_element_type=F32
                )
                top = jnp.max(s, axis=1, keepdims=True)
                e = jnp.exp2((s - top) * (128.0 ** -0.5 * LOG2E)).astype(BF)
                o = jnp.dot(e, jnp.concatenate([v[:, cut], count], axis=1), preferred_element_type=F32)
                mixed.append((o[:, :128] / o[:, 128:]).astype(BF))
            out[w + 1, :, cols] = jnp.concatenate(mixed, axis=1)
            return carry

        lax.fori_loop(0, 4, heads, 0, unroll=4)

    others = [(dy, dc) for dy in (2, 1, 3, 0) for dc in range(NC) if dy or dc]
    pair, odd = y // 2, lax.rem(y, 2)
    own_base, other_base = 3 * pair, 3 * (1 - pair)

    def z_step(f, k):
        if k == 1:
            own_piece(f).wait()
        else:
            z_copy(f, True, k - 1).wait_recv()
            z_copy(f, False, k - 1).wait_recv()
        go(z_copy(f, True, k))
        go(z_copy(f, False, k))

    def z_done(f):
        z_copy(f, True, 4).wait_recv()
        z_copy(f, False, 4).wait_recv()

    def x_step1(u):
        first_select(u)
        go(x_first(u, 0))
        go(x_first(u, 1))
        plain_select(u)
        go(x_second(u, 0, 1))
        go(x_second(u, 1, 0))
        if u in DIRECT:
            go(x_second(u, 0, 0))
            go(x_second(u, 1, 1))

    def x_step2(u):
        x_first(u, 0).wait_recv()
        x_first(u, 1).wait_recv()
        merge_select(u)
        go(x_second(u, 0, 0))
        go(x_second(u, 1, 1))

    def x_step3(u):
        for right in range(2):
            for half in range(2):
                x_second(u, right, half).wait_recv()
        if u in DIRECT:
            x_first(u, 0).wait_recv()
            x_first(u, 1).wait_recv()
        last_select(u)
        for dy, dc in others:
            go(a_copy(u, dy, dc))
        a_local(u).start()

    def w_start(pos):
        go(w_first(pos, 1))
        go(w_first((pos + 2) % 4, 0))

    def w_forward(pos):
        for right in (1, 0):
            unit = pos if right else (pos + 2) % 4
            w_first(unit, right).wait_recv()
            if pos < 2:
                go(w_second(unit))
            go(w_twin(unit, 3 if right else 1))

    def w_rest(n):
        for unit in (n, n + 2):
            w_second(unit).wait_recv()
            go(w_twin(unit, 2))

    def ids_ready():
        for dx in range(NX):
            for dc in range(NC):
                if dx or dc:
                    id_copy(dx, dc).wait_recv()
        copy = pltpu.make_async_copy(idv, ids_s, id_sem.at[0])
        copy.start()
        copy.wait()
        fill_table()

    def queries_ready():
        local[3].wait()
        h_query().wait_recv()
        shift_queries()

    def blocks_ready(shared):
        for u, unit in enumerate(UNITS):
            if unit[0] == shared:
                for dy, dc in others:
                    a_copy(u, dy, dc).wait_recv()
                a_local(u).wait()

    def e_send_both(m):
        go(e_first(m, 1))
        go(e_first(m, 0))

    def encode_own(stage):
        if stage == 0:
            blocks_ready(1)
            for rel in range(1, 4):
                for unit in range(4):
                    w_twin(unit, rel).wait_recv()
            for i in range(3):
                local[i].wait()
            first = nbp.at[pl.ds(0, 1)]
            encode_in(first, 1)
            encode_mix(1)
            encode_out(first, 1, [e_slot(0, 0)])
            e_send_both(0)
        rest = nbp.at[pl.ds(1, 2)]
        if stage == 1:
            encode_in(rest, 2)
        elif stage == 2:
            encode_mix(2)
        elif stage == 3:
            encode_out(rest, 2, [e_slot(1, 0), e_slot(2, 0)])
            e_send_both(1)
            e_send_both(2)

    def encode_common(i, stage):
        blocks = nbr.at[pl.ds(2 * i, 2)]
        if stage == 0:
            if i == 0:
                blocks_ready(0)
            encode_in(blocks, 2)
        elif stage == 1:
            encode_mix(2)
        else:
            encode_out(blocks, 2, [SHARED + 2 * i, SHARED + 2 * i + 1])

    def e_forward(m):
        if m != 1:
            e_first(m, 1).wait_recv()
            go(e_second(m, True))
        if m != 0:
            e_first(m, 0).wait_recv()
            go(e_second(m, False))

    def e_near():
        e_first(0, 0).wait_recv()
        e_first(1, 1).wait_recv()

    def attend_step(n):
        if n == 4:
            e_second(0, True).wait_recv()
            e_second(1, False).wait_recv()
        if n == 5:
            e_second(2, True).wait_recv()
            e_second(2, False).wait_recv()
        attend((
            own_base + 2 * odd, own_base + 2 * (1 - odd), other_base + 2 * (1 - odd), own_base + 1,
            other_base + 2 * odd, other_base + 1, 6, 7,
        )[n])

    def give_back():
        back_out[...] = out[8]
        go(h_back())

    steps = dict(
        z=z_step, zd=z_done, x1=x_step1, x2=x_step2, x3=x_step3, w0=w_start, wf=w_forward, wr=w_rest, q=queries_ready,
        ids=ids_ready, en=encode_own, er=encode_common, ef=e_forward, ar=e_near, at=attend_step, hb=give_back,
    )
    for dx in range(NX):
        for dc in range(NC):
            if dx or dc:
                go(id_copy(dx, dc))
    go(h_query())
    for name, *which in ORDER:
        steps[name](*which)
    h_back().wait_recv()
    out[0] = back_in[...]
    for copy in started:
        copy.wait_send()


def fused(ids, queries, database, norm_gain, enc_qkv, enc_out, out_gain, cca_kv):
    dma = pltpu.SemaphoreType.DMA
    NU = len(UNITS)
    def per_unit(*lead):
        return [
            pltpu.VMEM(lead + (SHARED // 2 if shared else 2, PART, WIDE * len(chunks)), BF)
            for shared, chunks in UNITS
        ]

    scratch = [pltpu.VMEM((NZ * BLOCKS, PART, WIDE), BF) for _ in range(NF)]
    scratch += per_unit(2, 2) + per_unit(2, 2) + per_unit(2, 2, 2) + per_unit(2, 2, 2)
    scratch += [
        pltpu.VMEM((2, SHARED if shared else 4, PART, WIDE * len(chunks)), BF) for shared, chunks in UNITS
    ]
    scratch += [
        pltpu.VMEM((8, 8, 128), jnp.int32),
        pltpu.SMEM((8, 8, 128), jnp.int32),
        pltpu.SMEM((2, 8, 16), jnp.int32),
        pltpu.VMEM((EACH, ROWS, D), BF),
        pltpu.VMEM((4, ROWS, D), BF),
        pltpu.VMEM((3, D, D), BF),
        pltpu.VMEM((D, D), BF),
        pltpu.VMEM((2, D, D), BF),
        pltpu.VMEM((SLOTS, ROWS, D), BF),
        pltpu.VMEM((8 * M, D), BF),
        pltpu.VMEM((M, D), BF),
        pltpu.VMEM((9, M, D), BF),
        pltpu.VMEM((M, D), BF),
        pltpu.VMEM((M, D), BF),
        pltpu.VMEM((2 * ROWS, D), BF),
        pltpu.VMEM((2 * ROWS, D), BF),
        pltpu.VMEM((2 * ROWS, D), F32),
        pltpu.VMEM((3, 2 * ROWS, D), BF),
        pltpu.VMEM((2, 2 * ROWS, D), BF),
        dma((16,)), dma((NF + 4,)), dma((NF, 8)), dma((NF, 8)), dma((NU, 6)), dma((NU, 6)),
        dma((NU, 8)), dma((NU, 8)), dma((NU,)),
        dma((12,)), dma((12,)), dma((12,)), dma((12,)), dma((10,)), dma((10,)), dma((2,)), dma((2,)),
    ]
    vmem = pl.BlockSpec(memory_space=pltpu.VMEM)
    hbm = pl.BlockSpec(memory_space=pl.ANY)
    return pl.pallas_call(
        body,
        out_shape=jax.ShapeDtypeStruct((9, M, D), BF),
        in_specs=[vmem, hbm, hbm, vmem, hbm, hbm, vmem, hbm],
        out_specs=vmem,
        scratch_shapes=scratch,
        compiler_params=pltpu.CompilerParams(
            collective_id=0, has_side_effects=True, vmem_limit_bytes=56 * 2**20
        ),
        cost_estimate=pl.CostEstimate(flops=14 * 10**9, bytes_accessed=12 * 2**20, transcendentals=4 * 10**6),
    )(ids, queries, database, norm_gain, enc_qkv, enc_out, out_gain, cca_kv)


def per_device(queries, database, nbr_ids, norm_gain, enc_qkv, enc_out, out_gain, cca_kv):
    groups = fused(
        nbr_ids.T, queries, database, norm_gain.reshape(8, 128), enc_qkv, enc_out, out_gain.reshape(8, 128), cca_kv
    )
    tokens = queries.shape[0]
    attended = groups.reshape(9 * M, D)[1 : tokens + 1]
    unserved = (lax.axis_index("seq") == 0) & (lax.broadcasted_iota(jnp.int32, (tokens, 1), 0) < M - 1)
    return jnp.where(unserved, jnp.zeros((), BF), attended)


def solution(mesh):
    placed = (
        P(("dp", "seq"), "tensor"),
        P("seq", None, None),
        P(("dp", "seq"), None),
        P(),
        P(None, None, "tensor"),
        P("tensor", None),
        P(),
        P(None, None, "tensor"),
    )
    return jax.shard_map(
        per_device,
        mesh=mesh,
        in_specs=placed,
        out_specs=P(("dp", "seq"), "tensor"),
        check_vma=False,
    )
```

```python
import functools

import jax
import jax.numpy as jnp
from jax import lax
from jax.experimental import pallas as pl
from jax.experimental.pallas import tpu as pltpu
from jax.sharding import PartitionSpec as P

NZ, NX, NY, NC = 8, 4, 4, 2
BLOCKS = 16
ROWS = 128
PART = 16
D = 1024
SLOTS = 16
M = 64
EPS = 1e-6
NF = 8
WIDE = D // NF
UNITS = ((1, (0, 1)), (1, (2, 3)), (1, (4, 5)), (1, (6, 7)), (0, (0, 1)), (0, (2, 3)), (0, (4, 5)), (0, (6, 7)))
SHARED = 8
EACH = SHARED // NY
HALF = 4
ORDER = (
    ('z', 5, 1), ('w0', 0), ('z', 2, 1), ('z', 3, 1), ('w0', 2), ('ids',),
    ('q',), ('z', 1, 1), ('w0', 1), ('z', 2, 2), ('z', 3, 2), ('z', 0, 1),
    ('z', 2, 3), ('wf', 0), ('z', 3, 3), ('z', 0, 2), ('z', 1, 2), ('z', 3, 4),
    ('z', 2, 4), ('z', 0, 3), ('z', 1, 3), ('qw', 3), ('z', 4, 1), ('w0', 3),
    ('zd', 3), ('zd', 2), ('z', 5, 2), ('x1', 1), ('x1', 5), ('wf', 1),
    ('z', 1, 4), ('z', 0, 4), ('z', 4, 2), ('z', 7, 1), ('qw', 0), ('x2', 1),
    ('zd', 1), ('wf', 2), ('z', 5, 3), ('x2', 5), ('zd', 0), ('z', 4, 3),
    ('x1', 4), ('z', 6, 1), ('z', 7, 2), ('x1', 0), ('z', 5, 4), ('x3', 5),
    ('x2', 4), ('z', 4, 4), ('z', 6, 2), ('x3', 1), ('x2', 0), ('z', 7, 3),
    ('zd', 5), ('wf', 3), ('zd', 4), ('x1', 6), ('z', 6, 3), ('x1', 2),
    ('x3', 4), ('wr', 1), ('z', 7, 4), ('x2', 6), ('z', 6, 4), ('x3', 0),
    ('x2', 2), ('zd', 6), ('zd', 7), ('x1', 3), ('x3', 6), ('x1', 7),
    ('x2', 3), ('x3', 2), ('qw', 1), ('x2', 7), ('qw', 2), ('wr', 0),
    ('x3', 3), ('x3', 7), ('en', 0), ('en', 1), ('en', 2), ('at', 0),
    ('er', 0, 0), ('er', 0, 1), ('er', 0, 2), ('er', 1, 0), ('er', 1, 1), ('er', 1, 2),
    ('ef', 0), ('ef', 1), ('er', 2, 0), ('er', 2, 1), ('er', 2, 2), ('at', 5),
    ('er', 3, 0), ('er', 3, 1), ('er', 3, 2), ('at', 7), ('hb',), ('at', 2),
    ('at', 3), ('at', 1), ('at', 4), ('at', 6),
)
LOG2E = 1.4426950408889634
BF = jnp.bfloat16
F32 = jnp.float32


def body(
    ids_in, queries, database, norm_gain, enc_qkv, enc_out, out_gain, cca_kv,
    out,
    *scratch,
):
    scratch = list(scratch)

    def take(n):
        got = scratch[:n]
        del scratch[:n]
        return got

    pool = take(NF)
    s1, r1, s2, r2, fin = (take(len(UNITS)) for _ in range(5))
    (
        idv, ids_s, table, nbp, nbr, wqkv, wout, wcca, enc, qraw, halo, qpad, back_out, back_in,
        normed, ctx, upd, qs, values, qw,
        id_sem, load_sem, z_send, z_recv, x_send, x_recv, a_send, a_recv, a_own,
        w_send, w_recv, b_send, b_recv, e_send, e_recv, h_send, h_recv,
    ) = scratch

    seq = lax.axis_index("seq")
    y = lax.axis_index("tensor")
    c = lax.axis_index("dp")
    z = seq // NX
    x = lax.rem(seq, NX)
    part = 2 * y + c

    def at(dz=0, dx=0, dy=0, dc=0):
        return {
            "seq": lax.rem(z + dz + NZ, NZ) * NX + lax.rem(x + dx + NX, NX),
            "tensor": lax.rem(y + dy + NY, NY),
            "dp": lax.rem(c + dc, NC),
        }

    def along(ds):
        return {"seq": lax.rem(seq + ds + NZ * NX, NZ * NX), "tensor": y, "dp": c}

    started = []

    def remote(src, dst, send_sem, recv_sem, device):
        return pltpu.make_async_remote_copy(
            src_ref=src, dst_ref=dst, send_sem=send_sem, recv_sem=recv_sem,
            device_id=device, device_id_type=pl.DeviceIdType.MESH,
        )

    def go(copy):
        copy.start()
        started.append(copy)

    def own_piece(f):
        return pltpu.make_async_copy(
            database.at[:, pl.ds(pl.multiple_of(PART * part, PART), PART), pl.ds(WIDE * f, WIDE)],
            pool[f].at[pl.ds(0, BLOCKS)], load_sem.at[f],
        )

    for f in range(NF):
        own_piece(f).start()
    ycol = pl.ds(pl.multiple_of(256 * y, 256), 256)
    local = [
        pltpu.make_async_copy(enc_qkv, wqkv.at[:, :, ycol], load_sem.at[NF]),
        pltpu.make_async_copy(enc_out, wout.at[ycol], load_sem.at[NF + 1]),
        pltpu.make_async_copy(cca_kv, wcca, load_sem.at[NF + 2]),
        pltpu.make_async_copy(queries, qraw, load_sem.at[NF + 3]),
    ]
    for copy in local:
        copy.start()
    idv[0] = jnp.zeros((8, 128), jnp.int32)
    idv[0, 0:2, 0:8] = ids_in[...]

    greet = [at(dz=1), at(dz=-1), along(1), along(-1)]
    greet += [at(dx=dx, dc=dc) for dx in range(NX) for dc in range(NC) if dx or dc]
    greet += [at(dy=dy, dc=dc) for dy in range(1, NY) for dc in range(NC)]
    barrier = pltpu.get_barrier_semaphore()
    for device in greet:
        pl.semaphore_signal(barrier, inc=1, device_id=device, device_id_type=pl.DeviceIdType.MESH)
    pl.semaphore_wait(barrier, len(greet))

    def z_copy(f, right, k):
        count = BLOCKS if k < 4 else BLOCKS // 2
        shift = 0 if (k < 4 or right) else BLOCKS // 2
        source = (k - 1) if right else (NZ - (k - 1)) % NZ
        target = k if right else NZ - k
        i = (k - 1) if right else 4 + (k - 1)
        return remote(
            pool[f].at[pl.ds(BLOCKS * source + shift, count)],
            pool[f].at[pl.ds(BLOCKS * target + shift, count)],
            z_send.at[f, i], z_recv.at[f, i], at(dz=1 if right else -1),
        )

    def id_copy(dx, dc):
        slot = ((NX - dx) % NX) * 2 + dc
        return remote(idv.at[0], idv.at[slot], id_sem.at[slot], id_sem.at[8 + slot], at(dx=dx, dc=dc))

    def x_first(u, half):
        return remote(
            s1[u].at[half], r1[u].at[half], x_send.at[u, half], x_recv.at[u, half],
            at(dx=-1 if half == 0 else 1),
        )

    def x_second(u, right, half):
        i = 2 + 2 * right + half
        return remote(
            s2[u].at[right, half], r2[u].at[right, half], x_send.at[u, i], x_recv.at[u, i],
            at(dx=1 if right else -1),
        )

    def a_ends(u, core, t):
        shared, chunks = UNITS[u]
        where = (
            slice(None), pl.ds(pl.multiple_of(PART * part, PART), PART),
            pl.ds(WIDE * chunks[0], WIDE * len(chunks)),
        )
        if shared:
            return fin[u].at[core, pl.ds(EACH * t, EACH)], nbp.at[where]
        return fin[u].at[core], nbr.at[where]

    def a_copy(u, dy, dc):
        i = dy * 2 + dc
        return remote(*a_ends(u, dc, lax.rem(y + dy, NY)), a_send.at[u, i], a_recv.at[u, i], at(dy=dy, dc=dc))

    def a_local(u):
        return pltpu.make_async_copy(*a_ends(u, 0, y), a_own.at[u])

    def w_place(unit, rel, of=None):
        t = lax.rem(y + rel + NY, NY)
        if unit < 3:
            return wqkv.at[unit, pl.ds(pl.multiple_of(512 * c, 512), 512), pl.ds(pl.multiple_of(256 * t, 256), 256)]
        return wout.at[pl.ds(pl.multiple_of(256 * t + 128 * c, 128), 128)]

    def w_own(unit):
        if unit < 3:
            return enc_qkv.at[unit, pl.ds(pl.multiple_of(512 * c, 512), 512)]
        return enc_out.at[pl.ds(pl.multiple_of(128 * c, 128), 128)]

    def w_first(unit, right):
        i = unit + 4 * right
        return remote(w_own(unit), w_place(unit, 0), w_send.at[i], w_recv.at[i], at(dy=1 if right else -1))

    def w_second(unit):
        right = unit < 2
        return remote(
            w_place(unit, -1 if right else 1), w_place(unit, -1 if right else 1),
            w_send.at[8 + unit], w_recv.at[8 + unit], at(dy=1 if right else -1),
        )

    def w_twin(unit, rel):
        i = unit + 4 * (rel - 1)
        return remote(w_place(unit, rel), w_place(unit, rel), b_send.at[i], b_recv.at[i], at(dc=1))

    def e_place(m, rel):
        return enc.at[2 * lax.rem(y + rel + NY, NY) + m]

    def e_first(m, right):
        i = 2 * m + right
        return remote(e_place(m, 0), e_place(m, 0), e_send.at[i], e_recv.at[i], at(dy=1 if right else -1))

    def e_second(m):
        rel = -1 if m == 0 else 1
        return remote(e_place(m, rel), e_place(m, rel), e_send.at[4 + m], e_recv.at[4 + m], at(dy=-rel))

    def h_query():
        return remote(queries.at[pl.ds(0, M)], halo, h_send.at[0], h_recv.at[0], along(-1))

    def h_back():
        return remote(back_out, back_in, h_send.at[1], h_recv.at[1], along(1))

    def fill_table():
        def step(q, carry):
            for p in range(SLOTS):
                b = ids_s[q, p % 2, p // 2]
                table[0, q, p] = ((z - (b >> 6) + NZ) & (NZ - 1)) * BLOCKS + (b & (BLOCKS - 1))
                table[1, q, p] = ((b >> 4) - x + NX) & (NX - 1)
            return carry

        lax.fori_loop(0, 8, step, 0)

    def each(u, act):
        shared, chunks = UNITS[u]
        first = 0 if shared else SHARED

        def step(i, carry):
            for core in range(2):
                for n, f in enumerate(chunks):
                    act(f, core, i, (first + i, first + HALF + i), slice(WIDE * n, WIDE * (n + 1)))
            return carry

        lax.fori_loop(0, HALF, step, 0, unroll=2)

    def mine(f, requester, core, p):
        return pool[f][table[0, 2 * requester + core, p]]

    def owner(requester, core, p):
        return table[1, 2 * requester + core, p]

    def first_select(u):
        def act(f, core, i, p, cols):
            for half in range(2):
                s1[u][half, core, i, :, cols] = mine(f, 2, core, p[half])

        each(u, act)

    def plain_select(u):
        def act(f, core, i, p, cols):
            s2[u][0, 1, core, i, :, cols] = mine(f, 3, core, p[1])
            s2[u][1, 0, core, i, :, cols] = mine(f, 1, core, p[0])

        each(u, act)

    def merge_select(u):
        def act(f, core, i, p, cols):
            s2[u][0, 0, core, i, :, cols] = jnp.where(
                owner(3, core, p[0]) == 0, mine(f, 3, core, p[0]), r1[u][0, core, i, :, cols]
            )
            s2[u][1, 1, core, i, :, cols] = jnp.where(
                owner(1, core, p[1]) == 0, mine(f, 1, core, p[1]), r1[u][1, core, i, :, cols]
            )

        each(u, act)

    def last_select(u):
        def act(f, core, i, p, cols):
            for half in range(2):
                of = owner(0, core, p[half])
                right, left = r2[u][0, half, core, i, :, cols], r2[u][1, half, core, i, :, cols]
                if half == 0:
                    far = jnp.where(of == 3, left, right)
                else:
                    far = jnp.where(of == 1, right, left)
                fin[u][core, half * HALF + i, :, cols] = jnp.where(of == 0, mine(f, 0, core, p[half]), far)

        each(u, act)

    def shift_queries():
        top = lax.broadcasted_iota(jnp.int32, (M, D), 0) == 0
        before = jnp.zeros((M, D), F32)
        for g in range(9):
            tile = qraw[pl.ds(M * g, M)] if g < 8 else halo[...]
            turned = pltpu.roll(tile.astype(F32), 1, 0)
            qpad[g] = jnp.where(top, before, turned).astype(BF)
            before = turned

    def gain(ref):
        g = ref[...].astype(F32)
        return jnp.concatenate([g[i : i + 1] for i in range(8)], axis=1)

    def encode_in(blocks, count):
        rows = pl.ds(0, count * ROWS)
        raw = blocks[...].reshape(count * ROWS, D).astype(F32)
        scale = lax.rsqrt(jnp.mean(raw * raw, axis=1, keepdims=True) + EPS)
        normed[rows] = (raw * scale * gain(norm_gain)).astype(BF)

        for j in range(3):
            qs[j, rows] = jnp.dot(normed[rows], wqkv[j], preferred_element_type=F32).astype(BF)

    def encode_mix(count):
        rows = pl.ds(0, count * ROWS)
        low = lax.broadcasted_iota(jnp.int32, (ROWS, 128), 1) < 64
        zero, one = jnp.zeros((ROWS, 128), BF), jnp.ones((ROWS, 128), BF)
        sums = jnp.concatenate([jnp.where(low, one, zero), jnp.where(low, zero, one)], axis=0)

        def heads(g, carry):
            cols = pl.ds(pl.multiple_of(256 * g, 256), 256)
            q, k, v = qs[0, rows, cols], qs[1, rows, cols], qs[2, rows, cols]
            mixed = []
            for n in range(count):
                pairs = []
                for p in range(2):
                    cut = (slice(ROWS * n, ROWS * (n + 1)), slice(128 * p, 128 * (p + 1)))
                    qp, kp, vp = q[cut], k[cut], v[cut]
                    k2 = jnp.concatenate([jnp.where(low, kp, zero), jnp.where(low, zero, kp)], axis=0)
                    v2 = jnp.concatenate([jnp.where(low, vp, zero), jnp.where(low, zero, vp)], axis=0)
                    s = lax.dot_general(qp, k2, (((1,), (1,)), ((), ())), preferred_element_type=F32)
                    probs = []
                    for h in range(2):
                        sh = s[:, 128 * h : 128 * (h + 1)]
                        top = jnp.max(sh, axis=1, keepdims=True)
                        probs.append(jnp.exp2((sh - top) * (0.125 * LOG2E)).astype(BF))
                    o = jnp.dot(
                        jnp.concatenate(probs, axis=1), jnp.concatenate([v2, sums], axis=1),
                        preferred_element_type=F32,
                    )
                    pairs.append((o[:, :128] / o[:, 128:]).astype(BF))
                mixed.append(jnp.concatenate(pairs, axis=1))
            ctx[rows, cols] = jnp.concatenate(mixed, axis=0)
            return carry

        lax.fori_loop(0, 4, heads, 0, unroll=4)

    def encode_out(blocks, count, places):
        rows = pl.ds(0, count * ROWS)

        upd[rows] = jnp.dot(ctx[rows], wout[...], preferred_element_type=F32)
        total = upd[rows] + blocks[...].reshape(count * ROWS, D).astype(F32)
        scale = lax.rsqrt(jnp.mean(total * total, axis=1, keepdims=True) + EPS)
        done = (total * scale * gain(out_gain)).astype(BF)
        for n, place in enumerate(places):
            enc[place] = done[ROWS * n : ROWS * (n + 1)]

    def fold_keys(i):
        rows = qpad[pl.ds(2 * i + 1, 2)].reshape(2 * M, D)
        for h in range(8):
            cut = slice(128 * h, 128 * (h + 1))
            folded = lax.dot_general(
                rows[:, cut], wcca[0, :, cut], (((1,), (1,)), ((), ())), preferred_element_type=F32
            ).astype(BF)
            qw[2 * i, M * h : M * (h + 1)] = folded[:M]
            qw[2 * i + 1, M * h : M * (h + 1)] = folded[M:]

    def attend(w):
        rows = enc[pl.ds(2 * w, 2)].reshape(2 * ROWS, D)
        s = lax.dot_general(qw[w], rows, (((1,), (1,)), ((), ())), preferred_element_type=F32)
        values[...] = jnp.dot(rows, wcca[1], preferred_element_type=F32).astype(BF)
        top = jnp.max(s, axis=1, keepdims=True)
        e = jnp.exp2((s - top) * (128.0 ** -0.5 * LOG2E)).astype(BF)
        sums = jnp.ones((2 * ROWS, 128), BF)
        for h in range(8):
            cut = slice(128 * h, 128 * (h + 1))
            o = jnp.dot(
                e[M * h : M * (h + 1)], jnp.concatenate([values[:, cut], sums], axis=1),
                preferred_element_type=F32,
            )
            out[w + 1, :, cut] = (o[:, :128] / o[:, 128:]).astype(BF)

    others = [(dy, dc) for dy in (2, 1, 3, 0) for dc in range(NC) if dy or dc]

    def z_step(f, k):
        if k == 1:
            own_piece(f).wait()
        else:
            z_copy(f, True, k - 1).wait_recv()
            z_copy(f, False, k - 1).wait_recv()
        go(z_copy(f, True, k))
        go(z_copy(f, False, k))

    def z_done(f):
        z_copy(f, True, 4).wait_recv()
        z_copy(f, False, 4).wait_recv()

    def x_step1(u):
        first_select(u)
        go(x_first(u, 0))
        go(x_first(u, 1))
        plain_select(u)
        go(x_second(u, 0, 1))
        go(x_second(u, 1, 0))

    def x_step2(u):
        x_first(u, 0).wait_recv()
        x_first(u, 1).wait_recv()
        merge_select(u)
        go(x_second(u, 0, 0))
        go(x_second(u, 1, 1))

    def x_step3(u):
        for right in range(2):
            for half in range(2):
                x_second(u, right, half).wait_recv()
        last_select(u)
        for dy, dc in others:
            go(a_copy(u, dy, dc))
        a_local(u).start()

    def w_start(pos):
        go(w_first(pos, 1))
        go(w_first((pos + 2) % 4, 0))

    def w_forward(pos):
        for right in (1, 0):
            unit = pos if right else (pos + 2) % 4
            w_first(unit, right).wait_recv()
            if pos < 2:
                go(w_second(unit))
            go(w_twin(unit, 3 if right else 1))

    def w_rest(n):
        for unit in (n, n + 2):
            w_second(unit).wait_recv()
            go(w_twin(unit, 2))

    def ids_ready():
        for dx in range(NX):
            for dc in range(NC):
                if dx or dc:
                    id_copy(dx, dc).wait_recv()
        copy = pltpu.make_async_copy(idv, ids_s, id_sem.at[0])
        copy.start()
        copy.wait()
        fill_table()

    def queries_ready():
        local[2].wait()
        local[3].wait()
        h_query().wait_recv()
        shift_queries()

    def blocks_ready(shared):
        for u, unit in enumerate(UNITS):
            if unit[0] == shared:
                for dy, dc in others:
                    a_copy(u, dy, dc).wait_recv()
                a_local(u).wait()

    def encode_own(stage):
        if stage == 0:
            blocks_ready(1)
            for rel in range(1, 4):
                for unit in range(4):
                    w_twin(unit, rel).wait_recv()
            for i in range(2):
                local[i].wait()
            encode_in(nbp, 2)
        elif stage == 1:
            encode_mix(2)
        else:
            encode_out(nbp, 2, [2 * y, 2 * y + 1])
            for m, right in ((0, 1), (1, 0), (1, 1), (0, 0)):
                go(e_first(m, right))

    def encode_common(i, stage):
        blocks = nbr.at[pl.ds(2 * i, 2)]
        if stage == 0:
            if i == 0:
                blocks_ready(0)
            encode_in(blocks, 2)
        elif stage == 1:
            encode_mix(2)
        else:
            encode_out(blocks, 2, [SHARED + 2 * i, SHARED + 2 * i + 1])

    def e_forward(m):
        e_first(m, 1 - m).wait_recv()
        go(e_second(m))

    def attend_step(n):
        if n == 1:
            e_first(1, 1).wait_recv()
        elif n == 2:
            e_first(0, 0).wait_recv()
        elif n == 3:
            e_second(0).wait_recv()
            e_second(1).wait_recv()
        attend((y, lax.rem(y + 3, NY), lax.rem(y + 1, NY), lax.rem(y + 2, NY), 4, 5, 6, 7)[n])

    def give_back():
        back_out[...] = out[8]
        go(h_back())

    steps = dict(
        z=z_step, zd=z_done, x1=x_step1, x2=x_step2, x3=x_step3, w0=w_start, wf=w_forward, wr=w_rest, q=queries_ready,
        qw=fold_keys, ids=ids_ready, en=encode_own, er=encode_common, ef=e_forward, at=attend_step, hb=give_back,
    )
    for dx in range(NX):
        for dc in range(NC):
            if dx or dc:
                go(id_copy(dx, dc))
    go(h_query())
    for name, *which in ORDER:
        steps[name](*which)
    h_back().wait_recv()
    out[0] = back_in[...]
    for copy in started:
        copy.wait_send()


def fused(ids, queries, database, norm_gain, enc_qkv, enc_out, out_gain, cca_kv):
    dma = pltpu.SemaphoreType.DMA
    NU = len(UNITS)
    def per_unit(*lead):
        return [
            pltpu.VMEM(lead + (HALF, PART, WIDE * len(chunks)), BF) for _, chunks in UNITS
        ]

    scratch = [pltpu.VMEM((NZ * BLOCKS, PART, WIDE), BF) for _ in range(NF)]
    scratch += per_unit(2, 2) + per_unit(2, 2) + per_unit(2, 2, 2) + per_unit(2, 2, 2)
    scratch += [
        pltpu.VMEM((2, 2 * HALF, PART, WIDE * len(chunks)), BF) for _, chunks in UNITS
    ]
    scratch += [
        pltpu.VMEM((8, 8, 128), jnp.int32),
        pltpu.SMEM((8, 8, 128), jnp.int32),
        pltpu.SMEM((2, 8, 16), jnp.int32),
        pltpu.VMEM((EACH, ROWS, D), BF),
        pltpu.VMEM((SLOTS - SHARED, ROWS, D), BF),
        pltpu.VMEM((3, D, D), BF),
        pltpu.VMEM((D, D), BF),
        pltpu.VMEM((2, D, D), BF),
        pltpu.VMEM((SLOTS, ROWS, D), BF),
        pltpu.VMEM((8 * M, D), BF),
        pltpu.VMEM((M, D), BF),
        pltpu.VMEM((9, M, D), BF),
        pltpu.VMEM((M, D), BF),
        pltpu.VMEM((M, D), BF),
        pltpu.VMEM((2 * ROWS, D), BF),
        pltpu.VMEM((2 * ROWS, D), BF),
        pltpu.VMEM((2 * ROWS, D), F32),
        pltpu.VMEM((3, 2 * ROWS, D), BF),
        pltpu.VMEM((2 * ROWS, D), BF),
        pltpu.VMEM((8, 8 * M, D), BF),
        dma((16,)), dma((NF + 4,)), dma((NF, 8)), dma((NF, 8)), dma((NU, 6)), dma((NU, 6)),
        dma((NU, 8)), dma((NU, 8)), dma((NU,)),
        dma((12,)), dma((12,)), dma((12,)), dma((12,)), dma((6,)), dma((6,)), dma((2,)), dma((2,)),
    ]
    vmem = pl.BlockSpec(memory_space=pltpu.VMEM)
    hbm = pl.BlockSpec(memory_space=pl.ANY)
    return pl.pallas_call(
        body,
        out_shape=jax.ShapeDtypeStruct((9, M, D), BF),
        in_specs=[vmem, hbm, hbm, vmem, hbm, hbm, vmem, hbm],
        out_specs=vmem,
        scratch_shapes=scratch,
        compiler_params=pltpu.CompilerParams(
            collective_id=0, has_side_effects=True, vmem_limit_bytes=60 * 2**20
        ),
        cost_estimate=pl.CostEstimate(flops=14 * 10**9, bytes_accessed=12 * 2**20, transcendentals=4 * 10**6),
    )(ids, queries, database, norm_gain, enc_qkv, enc_out, out_gain, cca_kv)


def per_device(queries, database, nbr_ids, norm_gain, enc_qkv, enc_out, out_gain, cca_kv):
    groups = fused(
        nbr_ids.T, queries, database, norm_gain.reshape(8, 128), enc_qkv, enc_out, out_gain.reshape(8, 128), cca_kv
    )
    tokens = queries.shape[0]
    attended = groups.reshape(9 * M, D)[1 : tokens + 1]
    unserved = (lax.axis_index("seq") == 0) & (lax.broadcasted_iota(jnp.int32, (tokens, 1), 0) < M - 1)
    return jnp.where(unserved, jnp.zeros((), BF), attended)


def solution(mesh):
    placed = (
        P(("dp", "seq"), "tensor"),
        P("seq", None, None),
        P(("dp", "seq"), None),
        P(),
        P(None, None, "tensor"),
        P("tensor", None),
        P(),
        P(None, None, "tensor"),
    )
    return jax.shard_map(
        per_device,
        mesh=mesh,
        in_specs=placed,
        out_specs=P(("dp", "seq"), "tensor"),
        check_vma=False,
    )
```

```python
import functools

import jax
import jax.numpy as jnp
from jax import lax
from jax.experimental import pallas as pl
from jax.experimental.pallas import tpu as pltpu
from jax.sharding import PartitionSpec as P

NZ, NX, NY, NC = 8, 4, 4, 2
BLOCKS = 16
ROWS = 128
PART = 16
D = 1024
SLOTS = 16
M = 64
EPS = 1e-6
NF = 8
WIDE = D // NF
UNITS = ((1, (0, 1)), (1, (2, 3)), (1, (4, 5)), (1, (6, 7)), (0, (0, 1)), (0, (2, 3)), (0, (4, 5)), (0, (6, 7)))
SHARED = 8
EACH = SHARED // NY
HALF = 4
ORDER = (
    ('z', 5, 1), ('w0', 0), ('z', 2, 1), ('g', 0), ('z', 3, 1), ('w0', 2),
    ('z', 1, 1), ('w0', 1), ('z', 2, 2), ('g', 1), ('z', 3, 2), ('z', 0, 1),
    ('g', 2), ('z', 2, 3), ('wf', 0), ('z', 3, 3), ('z', 0, 2), ('z', 1, 2),
    ('z', 3, 4), ('z', 2, 4), ('z', 0, 3), ('z', 1, 3), ('z', 4, 1), ('w0', 3),
    ('zd', 3), ('zd', 2), ('z', 5, 2), ('ids',), ('x1', 1), ('x1', 5),
    ('q',), ('qw', 0), ('wf', 1), ('z', 1, 4), ('z', 0, 4), ('z', 4, 2),
    ('z', 7, 1), ('x2', 1), ('zd', 1), ('wf', 2), ('z', 5, 3), ('x2', 5),
    ('zd', 0), ('z', 4, 3), ('x1', 4), ('qw', 1), ('z', 6, 1), ('z', 7, 2),
    ('x1', 0), ('qw', 2), ('z', 5, 4), ('x3', 5), ('x2', 4), ('z', 4, 4),
    ('z', 6, 2), ('x3', 1), ('x2', 0), ('z', 7, 3), ('zd', 5), ('wf', 3),
    ('zd', 4), ('x1', 6), ('qw', 3), ('z', 6, 3), ('x1', 2), ('x3', 4),
    ('wr', 1), ('z', 7, 4), ('x2', 6), ('z', 6, 4), ('x3', 0), ('x2', 2),
    ('zd', 6), ('zd', 7), ('x1', 3), ('x3', 6), ('x1', 7), ('x2', 3),
    ('x3', 2), ('x2', 7), ('wr', 0), ('x3', 3), ('x3', 7), ('en', 0),
    ('en', 1), ('en', 2), ('at', 0), ('er', 0, 0), ('er', 0, 1), ('er', 0, 2),
    ('er', 1, 0), ('er', 1, 1), ('er', 1, 2), ('ef', 0), ('ef', 1), ('er', 2, 0),
    ('er', 2, 1), ('er', 2, 2), ('at', 5), ('er', 3, 0), ('er', 3, 1), ('er', 3, 2),
    ('at', 7), ('hb',), ('at', 2), ('at', 3), ('at', 1), ('at', 4),
    ('at', 6),
)
LOG2E = 1.4426950408889634
BF = jnp.bfloat16
F32 = jnp.float32


def body(
    ids_in, queries, database, norm_gain, enc_qkv, enc_out, out_gain, cca_kv,
    out,
    *scratch,
):
    scratch = list(scratch)

    def take(n):
        got = scratch[:n]
        del scratch[:n]
        return got

    pool = take(NF)
    s1, r1, s2, r2, fin = (take(len(UNITS)) for _ in range(5))
    (
        idv, ids_s, table, nbp, nbr, wqkv, wout, wcca, enc, qraw, halo, qpad, back_out, back_in,
        normed, ctx, upd, qs, values, qw,
        id_sem, load_sem, z_send, z_recv, x_send, x_recv, a_send, a_recv, a_own,
        w_send, w_recv, b_send, b_recv, e_send, e_recv, h_send, h_recv, further,
    ) = scratch

    seq = lax.axis_index("seq")
    y = lax.axis_index("tensor")
    c = lax.axis_index("dp")
    z = seq // NX
    x = lax.rem(seq, NX)
    part = 2 * y + c

    def at(dz=0, dx=0, dy=0, dc=0):
        return {
            "seq": lax.rem(z + dz + NZ, NZ) * NX + lax.rem(x + dx + NX, NX),
            "tensor": lax.rem(y + dy + NY, NY),
            "dp": lax.rem(c + dc, NC),
        }

    def along(ds):
        return {"seq": lax.rem(seq + ds + NZ * NX, NZ * NX), "tensor": y, "dp": c}

    started = []

    def remote(src, dst, send_sem, recv_sem, device):
        return pltpu.make_async_remote_copy(
            src_ref=src, dst_ref=dst, send_sem=send_sem, recv_sem=recv_sem,
            device_id=device, device_id_type=pl.DeviceIdType.MESH,
        )

    def go(copy):
        copy.start()
        started.append(copy)

    def own_piece(f):
        return pltpu.make_async_copy(
            database.at[:, pl.ds(pl.multiple_of(PART * part, PART), PART), pl.ds(WIDE * f, WIDE)],
            pool[f].at[pl.ds(0, BLOCKS)], load_sem.at[f],
        )

    for f in range(NF):
        own_piece(f).start()
    ycol = pl.ds(pl.multiple_of(256 * y, 256), 256)
    local = [
        pltpu.make_async_copy(enc_qkv, wqkv.at[:, :, ycol], load_sem.at[NF]),
        pltpu.make_async_copy(enc_out, wout.at[ycol], load_sem.at[NF + 1]),
        pltpu.make_async_copy(cca_kv, wcca, load_sem.at[NF + 2]),
        pltpu.make_async_copy(queries, qraw, load_sem.at[NF + 3]),
    ]
    for copy in local:
        copy.start()
    idv[0] = jnp.zeros((8, 128), jnp.int32)
    idv[0, 0:2, 0:8] = ids_in[...]

    near = [at(dz=1), at(dz=-1), at(dx=1), at(dx=-1), at(dy=1), at(dy=-1), at(dc=1)]
    barrier = pltpu.get_barrier_semaphore()

    def greet(semaphore):
        for device in near:
            pl.semaphore_signal(semaphore, inc=1, device_id=device, device_id_type=pl.DeviceIdType.MESH)

    greet(barrier)
    pl.semaphore_wait(barrier, len(near))

    def greet_more(step):
        if step > 0:
            pl.semaphore_wait(further.at[step - 1], len(near))
        if step < 2:
            greet(further.at[step])
        else:
            for dx in range(NX):
                for dc in range(NC):
                    if dx or dc:
                        go(id_copy(dx, dc))
            go(h_query())

    def z_copy(f, right, k):
        count = BLOCKS if k < 4 else BLOCKS // 2
        shift = 0 if (k < 4 or right) else BLOCKS // 2
        source = (k - 1) if right else (NZ - (k - 1)) % NZ
        target = k if right else NZ - k
        i = (k - 1) if right else 4 + (k - 1)
        return remote(
            pool[f].at[pl.ds(BLOCKS * source + shift, count)],
            pool[f].at[pl.ds(BLOCKS * target + shift, count)],
            z_send.at[f, i], z_recv.at[f, i], at(dz=1 if right else -1),
        )

    def id_copy(dx, dc):
        slot = ((NX - dx) % NX) * 2 + dc
        return remote(idv.at[0], idv.at[slot], id_sem.at[slot], id_sem.at[8 + slot], at(dx=dx, dc=dc))

    def x_first(u, half):
        return remote(
            s1[u].at[half], r1[u].at[half], x_send.at[u, half], x_recv.at[u, half],
            at(dx=-1 if half == 0 else 1),
        )

    def x_second(u, right, half):
        i = 2 + 2 * right + half
        return remote(
            s2[u].at[right, half], r2[u].at[right, half], x_send.at[u, i], x_recv.at[u, i],
            at(dx=1 if right else -1),
        )

    def a_ends(u, core, t):
        shared, chunks = UNITS[u]
        where = (
            slice(None), pl.ds(pl.multiple_of(PART * part, PART), PART),
            pl.ds(WIDE * chunks[0], WIDE * len(chunks)),
        )
        if shared:
            return fin[u].at[core, pl.ds(EACH * t, EACH)], nbp.at[where]
        return fin[u].at[core], nbr.at[where]

    def a_copy(u, dy, dc):
        i = dy * 2 + dc
        return remote(*a_ends(u, dc, lax.rem(y + dy, NY)), a_send.at[u, i], a_recv.at[u, i], at(dy=dy, dc=dc))

    def a_local(u):
        return pltpu.make_async_copy(*a_ends(u, 0, y), a_own.at[u])

    def w_place(unit, rel, of=None):
        t = lax.rem(y + rel + NY, NY)
        if unit < 3:
            return wqkv.at[unit, pl.ds(pl.multiple_of(512 * c, 512), 512), pl.ds(pl.multiple_of(256 * t, 256), 256)]
        return wout.at[pl.ds(pl.multiple_of(256 * t + 128 * c, 128), 128)]

    def w_own(unit):
        if unit < 3:
            return enc_qkv.at[unit, pl.ds(pl.multiple_of(512 * c, 512), 512)]
        return enc_out.at[pl.ds(pl.multiple_of(128 * c, 128), 128)]

    def w_first(unit, right):
        i = unit + 4 * right
        return remote(w_own(unit), w_place(unit, 0), w_send.at[i], w_recv.at[i], at(dy=1 if right else -1))

    def w_second(unit):
        right = unit < 2
        return remote(
            w_place(unit, -1 if right else 1), w_place(unit, -1 if right else 1),
            w_send.at[8 + unit], w_recv.at[8 + unit], at(dy=1 if right else -1),
        )

    def w_twin(unit, rel):
        i = unit + 4 * (rel - 1)
        return remote(w_place(unit, rel), w_place(unit, rel), b_send.at[i], b_recv.at[i], at(dc=1))

    def e_place(m, rel):
        return enc.at[2 * lax.rem(y + rel + NY, NY) + m]

    def e_first(m, right):
        i = 2 * m + right
        return remote(e_place(m, 0), e_place(m, 0), e_send.at[i], e_recv.at[i], at(dy=1 if right else -1))

    def e_second(m):
        rel = -1 if m == 0 else 1
        return remote(e_place(m, rel), e_place(m, rel), e_send.at[4 + m], e_recv.at[4 + m], at(dy=-rel))

    def h_query():
        return remote(queries.at[pl.ds(0, M)], halo, h_send.at[0], h_recv.at[0], along(-1))

    def h_back():
        return remote(back_out, back_in, h_send.at[1], h_recv.at[1], along(1))

    def fill_table():
        def step(q, carry):
            for p in range(SLOTS):
                b = ids_s[q, p % 2, p // 2]
                table[0, q, p] = ((z - (b >> 6) + NZ) & (NZ - 1)) * BLOCKS + (b & (BLOCKS - 1))
                table[1, q, p] = ((b >> 4) - x + NX) & (NX - 1)
            return carry

        lax.fori_loop(0, 8, step, 0)

    def each(u, act):
        shared, chunks = UNITS[u]
        first = 0 if shared else SHARED

        def step(i, carry):
            for core in range(2):
                for n, f in enumerate(chunks):
                    act(f, core, i, (first + i, first + HALF + i), slice(WIDE * n, WIDE * (n + 1)))
            return carry

        lax.fori_loop(0, HALF, step, 0, unroll=2)

    def mine(f, requester, core, p):
        return pool[f][table[0, 2 * requester + core, p]]

    def owner(requester, core, p):
        return table[1, 2 * requester + core, p]

    def first_select(u):
        def act(f, core, i, p, cols):
            for half in range(2):
                s1[u][half, core, i, :, cols] = mine(f, 2, core, p[half])

        each(u, act)

    def plain_select(u):
        def act(f, core, i, p, cols):
            s2[u][0, 1, core, i, :, cols] = mine(f, 3, core, p[1])
            s2[u][1, 0, core, i, :, cols] = mine(f, 1, core, p[0])

        each(u, act)

    def merge_select(u):
        def act(f, core, i, p, cols):
            s2[u][0, 0, core, i, :, cols] = jnp.where(
                owner(3, core, p[0]) == 0, mine(f, 3, core, p[0]), r1[u][0, core, i, :, cols]
            )
            s2[u][1, 1, core, i, :, cols] = jnp.where(
                owner(1, core, p[1]) == 0, mine(f, 1, core, p[1]), r1[u][1, core, i, :, cols]
            )

        each(u, act)

    def last_select(u):
        def act(f, core, i, p, cols):
            for half in range(2):
                of = owner(0, core, p[half])
                right, left = r2[u][0, half, core, i, :, cols], r2[u][1, half, core, i, :, cols]
                if half == 0:
                    far = jnp.where(of == 3, left, right)
                else:
                    far = jnp.where(of == 1, right, left)
                fin[u][core, half * HALF + i, :, cols] = jnp.where(of == 0, mine(f, 0, core, p[half]), far)

        each(u, act)

    def shift_queries():
        top = lax.broadcasted_iota(jnp.int32, (M, D), 0) == 0
        before = jnp.zeros((M, D), F32)
        for g in range(9):
            tile = qraw[pl.ds(M * g, M)] if g < 8 else halo[...]
            turned = pltpu.roll(tile.astype(F32), 1, 0)
            qpad[g] = jnp.where(top, before, turned).astype(BF)
            before = turned

    def gain(ref):
        g = ref[...].astype(F32)
        return jnp.concatenate([g[i : i + 1] for i in range(8)], axis=1)

    def encode_in(blocks, count):
        rows = pl.ds(0, count * ROWS)
        raw = blocks[...].reshape(count * ROWS, D).astype(F32)
        scale = lax.rsqrt(jnp.mean(raw * raw, axis=1, keepdims=True) + EPS)
        normed[rows] = (raw * scale * gain(norm_gain)).astype(BF)

        for j in range(3):
            qs[j, rows] = jnp.dot(normed[rows], wqkv[j], preferred_element_type=F32).astype(BF)

    def encode_mix(count):
        rows = pl.ds(0, count * ROWS)
        low = lax.broadcasted_iota(jnp.int32, (ROWS, 128), 1) < 64
        zero, one = jnp.zeros((ROWS, 128), BF), jnp.ones((ROWS, 128), BF)
        sums = jnp.concatenate([jnp.where(low, one, zero), jnp.where(low, zero, one)], axis=0)

        def heads(g, carry):
            cols = pl.ds(pl.multiple_of(256 * g, 256), 256)
            q, k, v = qs[0, rows, cols], qs[1, rows, cols], qs[2, rows, cols]
            mixed = []
            for n in range(count):
                pairs = []
                for p in range(2):
                    cut = (slice(ROWS * n, ROWS * (n + 1)), slice(128 * p, 128 * (p + 1)))
                    qp, kp, vp = q[cut], k[cut], v[cut]
                    k2 = jnp.concatenate([jnp.where(low, kp, zero), jnp.where(low, zero, kp)], axis=0)
                    v2 = jnp.concatenate([jnp.where(low, vp, zero), jnp.where(low, zero, vp)], axis=0)
                    s = lax.dot_general(qp, k2, (((1,), (1,)), ((), ())), preferred_element_type=F32)
                    probs = []
                    for h in range(2):
                        sh = s[:, 128 * h : 128 * (h + 1)]
                        top = jnp.max(sh, axis=1, keepdims=True)
                        probs.append(jnp.exp2((sh - top) * (0.125 * LOG2E)).astype(BF))
                    o = jnp.dot(
                        jnp.concatenate(probs, axis=1), jnp.concatenate([v2, sums], axis=1),
                        preferred_element_type=F32,
                    )
                    pairs.append((o[:, :128] / o[:, 128:]).astype(BF))
                mixed.append(jnp.concatenate(pairs, axis=1))
            ctx[rows, cols] = jnp.concatenate(mixed, axis=0)
            return carry

        lax.fori_loop(0, 4, heads, 0, unroll=4)

    def encode_out(blocks, count, places):
        rows = pl.ds(0, count * ROWS)

        upd[rows] = jnp.dot(ctx[rows], wout[...], preferred_element_type=F32)
        total = upd[rows] + blocks[...].reshape(count * ROWS, D).astype(F32)
        scale = lax.rsqrt(jnp.mean(total * total, axis=1, keepdims=True) + EPS)
        done = (total * scale * gain(out_gain)).astype(BF)
        for n, place in enumerate(places):
            enc[place] = done[ROWS * n : ROWS * (n + 1)]

    def fold_keys(i):
        rows = qpad[pl.ds(2 * i + 1, 2)].reshape(2 * M, D)
        for h in range(8):
            cut = slice(128 * h, 128 * (h + 1))
            folded = lax.dot_general(
                rows[:, cut], wcca[0, :, cut], (((1,), (1,)), ((), ())), preferred_element_type=F32
            ).astype(BF)
            qw[2 * i, M * h : M * (h + 1)] = folded[:M]
            qw[2 * i + 1, M * h : M * (h + 1)] = folded[M:]

    def attend(w):
        rows = enc[pl.ds(2 * w, 2)].reshape(2 * ROWS, D)
        s = lax.dot_general(qw[w], rows, (((1,), (1,)), ((), ())), preferred_element_type=F32)
        values[...] = jnp.dot(rows, wcca[1], preferred_element_type=F32).astype(BF)
        top = jnp.max(s, axis=1, keepdims=True)
        e = jnp.exp2((s - top) * (128.0 ** -0.5 * LOG2E)).astype(BF)
        sums = jnp.ones((2 * ROWS, 128), BF)
        for h in range(8):
            cut = slice(128 * h, 128 * (h + 1))
            o = jnp.dot(
                e[M * h : M * (h + 1)], jnp.concatenate([values[:, cut], sums], axis=1),
                preferred_element_type=F32,
            )
            out[w + 1, :, cut] = (o[:, :128] / o[:, 128:]).astype(BF)

    others = [(dy, dc) for dy in (2, 1, 3, 0) for dc in range(NC) if dy or dc]

    def z_step(f, k):
        if k == 1:
            own_piece(f).wait()
        else:
            z_copy(f, True, k - 1).wait_recv()
            z_copy(f, False, k - 1).wait_recv()
        go(z_copy(f, True, k))
        go(z_copy(f, False, k))

    def z_done(f):
        z_copy(f, True, 4).wait_recv()
        z_copy(f, False, 4).wait_recv()

    def x_step1(u):
        first_select(u)
        go(x_first(u, 0))
        go(x_first(u, 1))
        plain_select(u)
        go(x_second(u, 0, 1))
        go(x_second(u, 1, 0))

    def x_step2(u):
        x_first(u, 0).wait_recv()
        x_first(u, 1).wait_recv()
        merge_select(u)
        go(x_second(u, 0, 0))
        go(x_second(u, 1, 1))

    def x_step3(u):
        for right in range(2):
            for half in range(2):
                x_second(u, right, half).wait_recv()
        last_select(u)
        for dy, dc in others:
            go(a_copy(u, dy, dc))
        a_local(u).start()

    def w_start(pos):
        go(w_first(pos, 1))
        go(w_first((pos + 2) % 4, 0))

    def w_forward(pos):
        for right in (1, 0):
            unit = pos if right else (pos + 2) % 4
            w_first(unit, right).wait_recv()
            if pos < 2:
                go(w_second(unit))
            go(w_twin(unit, 3 if right else 1))

    def w_rest(n):
        for unit in (n, n + 2):
            w_second(unit).wait_recv()
            go(w_twin(unit, 2))

    def ids_ready():
        for dx in range(NX):
            for dc in range(NC):
                if dx or dc:
                    id_copy(dx, dc).wait_recv()
        copy = pltpu.make_async_copy(idv, ids_s, id_sem.at[0])
        copy.start()
        copy.wait()
        fill_table()

    def queries_ready():
        local[2].wait()
        local[3].wait()
        h_query().wait_recv()
        shift_queries()

    def blocks_ready(shared):
        for u, unit in enumerate(UNITS):
            if unit[0] == shared:
                for dy, dc in others:
                    a_copy(u, dy, dc).wait_recv()
                a_local(u).wait()

    def encode_own(stage):
        if stage == 0:
            blocks_ready(1)
            for rel in range(1, 4):
                for unit in range(4):
                    w_twin(unit, rel).wait_recv()
            for i in range(2):
                local[i].wait()
            encode_in(nbp, 2)
        elif stage == 1:
            encode_mix(2)
        else:
            encode_out(nbp, 2, [2 * y, 2 * y + 1])
            for m, right in ((0, 1), (1, 0), (1, 1), (0, 0)):
                go(e_first(m, right))

    def encode_common(i, stage):
        blocks = nbr.at[pl.ds(2 * i, 2)]
        if stage == 0:
            if i == 0:
                blocks_ready(0)
            encode_in(blocks, 2)
        elif stage == 1:
            encode_mix(2)
        else:
            encode_out(blocks, 2, [SHARED + 2 * i, SHARED + 2 * i + 1])

    def e_forward(m):
        e_first(m, 1 - m).wait_recv()
        go(e_second(m))

    def attend_step(n):
        if n == 1:
            e_first(1, 1).wait_recv()
        elif n == 2:
            e_first(0, 0).wait_recv()
        elif n == 3:
            e_second(0).wait_recv()
            e_second(1).wait_recv()
        attend((y, lax.rem(y + 3, NY), lax.rem(y + 1, NY), lax.rem(y + 2, NY), 4, 5, 6, 7)[n])

    def give_back():
        back_out[...] = out[8]
        go(h_back())

    steps = dict(
        z=z_step, zd=z_done, x1=x_step1, x2=x_step2, x3=x_step3, w0=w_start, wf=w_forward, wr=w_rest, q=queries_ready,
        qw=fold_keys, ids=ids_ready, g=greet_more, en=encode_own, er=encode_common, ef=e_forward, at=attend_step, hb=give_back,
    )
    for name, *which in ORDER:
        steps[name](*which)
    h_back().wait_recv()
    out[0] = back_in[...]
    for copy in started:
        copy.wait_send()


def fused(ids, queries, database, norm_gain, enc_qkv, enc_out, out_gain, cca_kv):
    dma = pltpu.SemaphoreType.DMA
    NU = len(UNITS)
    def per_unit(*lead):
        return [
            pltpu.VMEM(lead + (HALF, PART, WIDE * len(chunks)), BF) for _, chunks in UNITS
        ]

    scratch = [pltpu.VMEM((NZ * BLOCKS, PART, WIDE), BF) for _ in range(NF)]
    scratch += per_unit(2, 2) + per_unit(2, 2) + per_unit(2, 2, 2) + per_unit(2, 2, 2)
    scratch += [
        pltpu.VMEM((2, 2 * HALF, PART, WIDE * len(chunks)), BF) for _, chunks in UNITS
    ]
    scratch += [
        pltpu.VMEM((8, 8, 128), jnp.int32),
        pltpu.SMEM((8, 8, 128), jnp.int32),
        pltpu.SMEM((2, 8, 16), jnp.int32),
        pltpu.VMEM((EACH, ROWS, D), BF),
        pltpu.VMEM((SLOTS - SHARED, ROWS, D), BF),
        pltpu.VMEM((3, D, D), BF),
        pltpu.VMEM((D, D), BF),
        pltpu.VMEM((2, D, D), BF),
        pltpu.VMEM((SLOTS, ROWS, D), BF),
        pltpu.VMEM((8 * M, D), BF),
        pltpu.VMEM((M, D), BF),
        pltpu.VMEM((9, M, D), BF),
        pltpu.VMEM((M, D), BF),
        pltpu.VMEM((M, D), BF),
        pltpu.VMEM((2 * ROWS, D), BF),
        pltpu.VMEM((2 * ROWS, D), BF),
        pltpu.VMEM((2 * ROWS, D), F32),
        pltpu.VMEM((3, 2 * ROWS, D), BF),
        pltpu.VMEM((2 * ROWS, D), BF),
        pltpu.VMEM((8, 8 * M, D), BF),
        dma((16,)), dma((NF + 4,)), dma((NF, 8)), dma((NF, 8)), dma((NU, 6)), dma((NU, 6)),
        dma((NU, 8)), dma((NU, 8)), dma((NU,)),
        dma((12,)), dma((12,)), dma((12,)), dma((12,)), dma((6,)), dma((6,)), dma((2,)), dma((2,)),
        pltpu.SemaphoreType.REGULAR((2,)),
    ]
    vmem = pl.BlockSpec(memory_space=pltpu.VMEM)
    hbm = pl.BlockSpec(memory_space=pl.ANY)
    return pl.pallas_call(
        body,
        out_shape=jax.ShapeDtypeStruct((9, M, D), BF),
        in_specs=[vmem, hbm, hbm, vmem, hbm, hbm, vmem, hbm],
        out_specs=vmem,
        scratch_shapes=scratch,
        compiler_params=pltpu.CompilerParams(
            collective_id=0, has_side_effects=True, vmem_limit_bytes=60 * 2**20
        ),
        cost_estimate=pl.CostEstimate(flops=14 * 10**9, bytes_accessed=12 * 2**20, transcendentals=4 * 10**6),
    )(ids, queries, database, norm_gain, enc_qkv, enc_out, out_gain, cca_kv)


def per_device(queries, database, nbr_ids, norm_gain, enc_qkv, enc_out, out_gain, cca_kv):
    groups = fused(
        nbr_ids.T, queries, database, norm_gain.reshape(8, 128), enc_qkv, enc_out, out_gain.reshape(8, 128), cca_kv
    )
    tokens = queries.shape[0]
    attended = groups.reshape(9 * M, D)[1 : tokens + 1]
    unserved = (lax.axis_index("seq") == 0) & (lax.broadcasted_iota(jnp.int32, (tokens, 1), 0) < M - 1)
    return jnp.where(unserved, jnp.zeros((), BF), attended)


def solution(mesh):
    placed = (
        P(("dp", "seq"), "tensor"),
        P("seq", None, None),
        P(("dp", "seq"), None),
        P(),
        P(None, None, "tensor"),
        P("tensor", None),
        P(),
        P(None, None, "tensor"),
    )
    return jax.shard_map(
        per_device,
        mesh=mesh,
        in_specs=placed,
        out_specs=P(("dp", "seq"), "tensor"),
        check_vma=False,
    )
```

```python
import functools

import jax
import jax.numpy as jnp
from jax import lax
from jax.experimental import pallas as pl
from jax.experimental.pallas import tpu as pltpu
from jax.sharding import PartitionSpec as P

NZ, NX, NY, NC = 8, 4, 4, 2
BLOCKS = 16
ROWS = 128
PART = 16
D = 1024
SLOTS = 16
M = 64
EPS = 1e-6
NF = 8
WIDE = D // NF
UNITS = ((1, (0, 1)), (1, (2, 3)), (1, (4, 5)), (1, (6, 7)), (0, (0, 1)), (0, (2, 3)), (0, (4, 5)), (0, (6, 7)))
SHARED = 8
EACH = SHARED // NY
HALF = 4
ORDER = (
    ('z', 5, 1), ('w0', 0), ('z', 2, 1), ('g', 0), ('z', 3, 1), ('w0', 2),
    ('z', 1, 1), ('w0', 1), ('z', 2, 2), ('g', 1), ('z', 3, 2), ('z', 0, 1),
    ('g', 2), ('z', 2, 3), ('wf', 0), ('z', 3, 3), ('z', 0, 2), ('z', 1, 2),
    ('z', 3, 4), ('z', 2, 4), ('z', 0, 3), ('z', 1, 3), ('z', 4, 1), ('w0', 3),
    ('zd', 3), ('zd', 2), ('z', 5, 2), ('ids',), ('x1', 1), ('x1', 5),
    ('q',), ('qw', 0), ('wf', 1), ('z', 1, 4), ('z', 0, 4), ('z', 4, 2),
    ('z', 7, 1), ('x2', 1), ('zd', 1), ('wf', 2), ('z', 5, 3), ('x2', 5),
    ('zd', 0), ('z', 4, 3), ('x1', 4), ('qw', 1), ('z', 6, 1), ('z', 7, 2),
    ('x1', 0), ('qw', 2), ('z', 5, 4), ('x3', 5), ('x2', 4), ('z', 4, 4),
    ('z', 6, 2), ('x3', 1), ('x2', 0), ('z', 7, 3), ('zd', 5), ('wf', 3),
    ('zd', 4), ('x1', 6), ('qw', 3), ('z', 6, 3), ('x1', 2), ('x3', 4),
    ('wr', 1), ('z', 7, 4), ('x2', 6), ('z', 6, 4), ('x3', 0), ('x2', 2),
    ('zd', 6), ('zd', 7), ('x1', 3), ('x1', 7), ('x3', 6), ('x2', 3),
    ('x2', 7), ('x3', 2), ('wr', 0), ('x3', 3), ('x3', 7), ('en', 0),
    ('en', 1), ('en', 2), ('at', 0), ('er', 0, 0), ('er', 0, 1), ('er', 0, 2),
    ('er', 1, 0), ('er', 1, 1), ('er', 1, 2), ('ef', 0), ('ef', 1), ('er', 2, 0),
    ('er', 2, 1), ('er', 2, 2), ('at', 5), ('er', 3, 0), ('er', 3, 1), ('er', 3, 2),
    ('at', 7), ('hb',), ('at', 2), ('at', 3), ('at', 1), ('at', 4),
    ('at', 6),
)
LOG2E = 1.4426950408889634
BF = jnp.bfloat16
F32 = jnp.float32


def body(
    ids_in, queries, database, norm_gain, enc_qkv, enc_out, out_gain, cca_kv,
    out,
    *scratch,
):
    scratch = list(scratch)

    def take(n):
        got = scratch[:n]
        del scratch[:n]
        return got

    pool = take(NF)
    s1, r1, s2, r2, fin = (take(len(UNITS)) for _ in range(5))
    (
        idv, ids_s, table, nbp, nbr, wqkv, wout, wcca, enc, qraw, halo, qpad, back_out, back_in,
        normed, ctx, upd, qs, values, qw,
        id_sem, load_sem, z_send, z_recv, x_send, x_recv, a_send, a_recv, a_own,
        w_send, w_recv, b_send, b_recv, e_send, e_recv, h_send, h_recv, further,
    ) = scratch

    seq = lax.axis_index("seq")
    y = lax.axis_index("tensor")
    c = lax.axis_index("dp")
    z = seq // NX
    x = lax.rem(seq, NX)
    part = 2 * y + c

    def at(dz=0, dx=0, dy=0, dc=0):
        return {
            "seq": lax.rem(z + dz + NZ, NZ) * NX + lax.rem(x + dx + NX, NX),
            "tensor": lax.rem(y + dy + NY, NY),
            "dp": lax.rem(c + dc, NC),
        }

    def along(ds):
        return {"seq": lax.rem(seq + ds + NZ * NX, NZ * NX), "tensor": y, "dp": c}

    started = []

    def remote(src, dst, send_sem, recv_sem, device):
        return pltpu.make_async_remote_copy(
            src_ref=src, dst_ref=dst, send_sem=send_sem, recv_sem=recv_sem,
            device_id=device, device_id_type=pl.DeviceIdType.MESH,
        )

    def go(copy):
        copy.start()
        started.append(copy)

    def own_piece(f):
        return pltpu.make_async_copy(
            database.at[:, pl.ds(pl.multiple_of(PART * part, PART), PART), pl.ds(WIDE * f, WIDE)],
            pool[f].at[pl.ds(0, BLOCKS)], load_sem.at[f],
        )

    for f in range(NF):
        own_piece(f).start()
    ycol = pl.ds(pl.multiple_of(256 * y, 256), 256)
    local = [
        pltpu.make_async_copy(enc_qkv, wqkv.at[:, :, ycol], load_sem.at[NF]),
        pltpu.make_async_copy(enc_out, wout.at[ycol], load_sem.at[NF + 1]),
        pltpu.make_async_copy(cca_kv, wcca, load_sem.at[NF + 2]),
        pltpu.make_async_copy(queries, qraw, load_sem.at[NF + 3]),
    ]
    for copy in local:
        copy.start()
    idv[0] = jnp.zeros((8, 128), jnp.int32)
    idv[0, 0:2, 0:8] = ids_in[...]

    near = [at(dz=1), at(dz=-1), at(dx=1), at(dx=-1), at(dy=1), at(dy=-1), at(dc=1)]
    barrier = pltpu.get_barrier_semaphore()

    def greet(semaphore):
        for device in near:
            pl.semaphore_signal(semaphore, inc=1, device_id=device, device_id_type=pl.DeviceIdType.MESH)

    greet(barrier)
    pl.semaphore_wait(barrier, len(near))

    def greet_more(step):
        if step > 0:
            pl.semaphore_wait(further.at[step - 1], len(near))
        if step < 2:
            greet(further.at[step])
        else:
            for dx in range(NX):
                for dc in range(NC):
                    if dx or dc:
                        go(id_copy(dx, dc))
            go(h_query())

    def z_copy(f, right, k):
        count = BLOCKS if k < 4 else BLOCKS // 2
        shift = 0 if (k < 4 or right) else BLOCKS // 2
        source = (k - 1) if right else (NZ - (k - 1)) % NZ
        target = k if right else NZ - k
        i = (k - 1) if right else 4 + (k - 1)
        return remote(
            pool[f].at[pl.ds(BLOCKS * source + shift, count)],
            pool[f].at[pl.ds(BLOCKS * target + shift, count)],
            z_send.at[f, i], z_recv.at[f, i], at(dz=1 if right else -1),
        )

    def id_copy(dx, dc):
        slot = ((NX - dx) % NX) * 2 + dc
        return remote(idv.at[0], idv.at[slot], id_sem.at[slot], id_sem.at[8 + slot], at(dx=dx, dc=dc))

    def x_first(u, half):
        return remote(
            s1[u].at[half], r1[u].at[half], x_send.at[u, half], x_recv.at[u, half],
            at(dx=-1 if half == 0 else 1),
        )

    def x_second(u, right, half):
        i = 2 + 2 * right + half
        return remote(
            s2[u].at[right, half], r2[u].at[right, half], x_send.at[u, i], x_recv.at[u, i],
            at(dx=1 if right else -1),
        )

    def a_ends(u, core, t):
        shared, chunks = UNITS[u]
        where = (
            slice(None), pl.ds(pl.multiple_of(PART * part, PART), PART),
            pl.ds(WIDE * chunks[0], WIDE * len(chunks)),
        )
        if shared:
            return fin[u].at[core, pl.ds(EACH * t, EACH)], nbp.at[where]
        return fin[u].at[core], nbr.at[where]

    def a_copy(u, dy, dc):
        i = dy * 2 + dc
        return remote(*a_ends(u, dc, lax.rem(y + dy, NY)), a_send.at[u, i], a_recv.at[u, i], at(dy=dy, dc=dc))

    def a_local(u):
        return pltpu.make_async_copy(*a_ends(u, 0, y), a_own.at[u])

    def w_place(unit, rel, of=None):
        t = lax.rem(y + rel + NY, NY)
        if unit < 3:
            return wqkv.at[unit, pl.ds(pl.multiple_of(512 * c, 512), 512), pl.ds(pl.multiple_of(256 * t, 256), 256)]
        return wout.at[pl.ds(pl.multiple_of(256 * t + 128 * c, 128), 128)]

    def w_own(unit):
        if unit < 3:
            return enc_qkv.at[unit, pl.ds(pl.multiple_of(512 * c, 512), 512)]
        return enc_out.at[pl.ds(pl.multiple_of(128 * c, 128), 128)]

    def w_first(unit, right):
        i = unit + 4 * right
        return remote(w_own(unit), w_place(unit, 0), w_send.at[i], w_recv.at[i], at(dy=1 if right else -1))

    def w_second(unit):
        right = unit < 2
        return remote(
            w_place(unit, -1 if right else 1), w_place(unit, -1 if right else 1),
            w_send.at[8 + unit], w_recv.at[8 + unit], at(dy=1 if right else -1),
        )

    def w_twin(unit, rel):
        i = unit + 4 * (rel - 1)
        return remote(w_place(unit, rel), w_place(unit, rel), b_send.at[i], b_recv.at[i], at(dc=1))

    def e_place(m, rel):
        return enc.at[2 * lax.rem(y + rel + NY, NY) + m]

    def e_first(m, right):
        i = 2 * m + right
        return remote(e_place(m, 0), e_place(m, 0), e_send.at[i], e_recv.at[i], at(dy=1 if right else -1))

    def e_second(m):
        rel = -1 if m == 0 else 1
        return remote(e_place(m, rel), e_place(m, rel), e_send.at[4 + m], e_recv.at[4 + m], at(dy=-rel))

    def h_query():
        return remote(queries.at[pl.ds(0, M)], halo, h_send.at[0], h_recv.at[0], along(-1))

    def h_back():
        return remote(back_out, back_in, h_send.at[1], h_recv.at[1], along(1))

    def fill_table():
        def step(q, carry):
            for p in range(SLOTS):
                b = ids_s[q, p % 2, p // 2]
                table[0, q, p] = ((z - (b >> 6) + NZ) & (NZ - 1)) * BLOCKS + (b & (BLOCKS - 1))
                table[1, q, p] = ((b >> 4) - x + NX) & (NX - 1)
            return carry

        lax.fori_loop(0, 8, step, 0)

    def each(u, act):
        shared, chunks = UNITS[u]
        first = 0 if shared else SHARED

        def step(i, carry):
            for core in range(2):
                for n, f in enumerate(chunks):
                    act(f, core, i, (first + i, first + HALF + i), slice(WIDE * n, WIDE * (n + 1)))
            return carry

        lax.fori_loop(0, HALF, step, 0, unroll=2)

    def mine(f, requester, core, p):
        return pool[f][table[0, 2 * requester + core, p]]

    def owner(requester, core, p):
        return table[1, 2 * requester + core, p]

    def first_select(u):
        def act(f, core, i, p, cols):
            for half in range(2):
                s1[u][half, core, i, :, cols] = mine(f, 2, core, p[half])

        each(u, act)

    def plain_select(u):
        def act(f, core, i, p, cols):
            s2[u][0, 1, core, i, :, cols] = mine(f, 3, core, p[1])
            s2[u][1, 0, core, i, :, cols] = mine(f, 1, core, p[0])

        each(u, act)

    def merge_select(u):
        def act(f, core, i, p, cols):
            s2[u][0, 0, core, i, :, cols] = jnp.where(
                owner(3, core, p[0]) == 0, mine(f, 3, core, p[0]), r1[u][0, core, i, :, cols]
            )
            s2[u][1, 1, core, i, :, cols] = jnp.where(
                owner(1, core, p[1]) == 0, mine(f, 1, core, p[1]), r1[u][1, core, i, :, cols]
            )

        each(u, act)

    def last_select(u):
        def act(f, core, i, p, cols):
            for half in range(2):
                of = owner(0, core, p[half])
                right, left = r2[u][0, half, core, i, :, cols], r2[u][1, half, core, i, :, cols]
                if half == 0:
                    far = jnp.where(of == 3, left, right)
                else:
                    far = jnp.where(of == 1, right, left)
                fin[u][core, half * HALF + i, :, cols] = jnp.where(of == 0, mine(f, 0, core, p[half]), far)

        each(u, act)

    def shift_queries():
        top = lax.broadcasted_iota(jnp.int32, (M, D), 0) == 0
        before = jnp.zeros((M, D), F32)
        for g in range(9):
            tile = qraw[pl.ds(M * g, M)] if g < 8 else halo[...]
            turned = pltpu.roll(tile.astype(F32), 1, 0)
            qpad[g] = jnp.where(top, before, turned).astype(BF)
            before = turned

    def gain(ref):
        g = ref[...].astype(F32)
        return jnp.concatenate([g[i : i + 1] for i in range(8)], axis=1)

    def encode_in(blocks, count):
        rows = pl.ds(0, count * ROWS)
        raw = blocks[...].reshape(count * ROWS, D).astype(F32)
        scale = lax.rsqrt(jnp.mean(raw * raw, axis=1, keepdims=True) + EPS)
        normed[rows] = (raw * scale * gain(norm_gain)).astype(BF)

        for j in range(3):
            qs[j, rows] = jnp.dot(normed[rows], wqkv[j], preferred_element_type=F32).astype(BF)

    def encode_mix(count):
        rows = pl.ds(0, count * ROWS)
        low = lax.broadcasted_iota(jnp.int32, (ROWS, 128), 1) < 64
        zero, one = jnp.zeros((ROWS, 128), BF), jnp.ones((ROWS, 128), BF)
        sums = jnp.concatenate([jnp.where(low, one, zero), jnp.where(low, zero, one)], axis=0)

        def heads(g, carry):
            cols = pl.ds(pl.multiple_of(256 * g, 256), 256)
            q, k, v = qs[0, rows, cols], qs[1, rows, cols], qs[2, rows, cols]
            mixed = []
            for n in range(count):
                pairs = []
                for p in range(2):
                    cut = (slice(ROWS * n, ROWS * (n + 1)), slice(128 * p, 128 * (p + 1)))
                    qp, kp, vp = q[cut], k[cut], v[cut]
                    k2 = jnp.concatenate([jnp.where(low, kp, zero), jnp.where(low, zero, kp)], axis=0)
                    v2 = jnp.concatenate([jnp.where(low, vp, zero), jnp.where(low, zero, vp)], axis=0)
                    s = lax.dot_general(qp, k2, (((1,), (1,)), ((), ())), preferred_element_type=F32)
                    probs = []
                    for h in range(2):
                        sh = s[:, 128 * h : 128 * (h + 1)]
                        top = jnp.max(sh, axis=1, keepdims=True)
                        probs.append(jnp.exp2((sh - top) * (0.125 * LOG2E)).astype(BF))
                    o = jnp.dot(
                        jnp.concatenate(probs, axis=1), jnp.concatenate([v2, sums], axis=1),
                        preferred_element_type=F32,
                    )
                    pairs.append((o[:, :128] / o[:, 128:]).astype(BF))
                mixed.append(jnp.concatenate(pairs, axis=1))
            ctx[rows, cols] = jnp.concatenate(mixed, axis=0)
            return carry

        lax.fori_loop(0, 4, heads, 0, unroll=4)

    def encode_out(blocks, count, places):
        rows = pl.ds(0, count * ROWS)

        upd[rows] = jnp.dot(ctx[rows], wout[...], preferred_element_type=F32)
        total = upd[rows] + blocks[...].reshape(count * ROWS, D).astype(F32)
        scale = lax.rsqrt(jnp.mean(total * total, axis=1, keepdims=True) + EPS)
        done = (total * scale * gain(out_gain)).astype(BF)
        for n, place in enumerate(places):
            enc[place] = done[ROWS * n : ROWS * (n + 1)]

    def fold_keys(i):
        rows = qpad[pl.ds(2 * i + 1, 2)].reshape(2 * M, D)
        for h in range(8):
            cut = slice(128 * h, 128 * (h + 1))
            folded = lax.dot_general(
                rows[:, cut], wcca[0, :, cut], (((1,), (1,)), ((), ())), preferred_element_type=F32
            ).astype(BF)
            qw[2 * i, M * h : M * (h + 1)] = folded[:M]
            qw[2 * i + 1, M * h : M * (h + 1)] = folded[M:]

    def attend(w):
        rows = enc[pl.ds(2 * w, 2)].reshape(2 * ROWS, D)
        s = lax.dot_general(qw[w], rows, (((1,), (1,)), ((), ())), preferred_element_type=F32)
        values[...] = jnp.dot(rows, wcca[1], preferred_element_type=F32).astype(BF)
        top = jnp.max(s, axis=1, keepdims=True)
        e = jnp.exp2((s - top) * (128.0 ** -0.5 * LOG2E)).astype(BF)
        sums = jnp.ones((2 * ROWS, 128), BF)
        for h in range(8):
            cut = slice(128 * h, 128 * (h + 1))
            o = jnp.dot(
                e[M * h : M * (h + 1)], jnp.concatenate([values[:, cut], sums], axis=1),
                preferred_element_type=F32,
            )
            out[w + 1, :, cut] = (o[:, :128] / o[:, 128:]).astype(BF)

    others = [(dy, dc) for dy in (2, 1, 3, 0) for dc in range(NC) if dy or dc]

    def z_step(f, k):
        if k == 1:
            own_piece(f).wait()
        else:
            z_copy(f, True, k - 1).wait_recv()
            z_copy(f, False, k - 1).wait_recv()
        go(z_copy(f, True, k))
        go(z_copy(f, False, k))

    def z_done(f):
        z_copy(f, True, 4).wait_recv()
        z_copy(f, False, 4).wait_recv()

    def x_step1(u):
        first_select(u)
        go(x_first(u, 0))
        go(x_first(u, 1))
        plain_select(u)
        go(x_second(u, 0, 1))
        go(x_second(u, 1, 0))

    def x_step2(u):
        x_first(u, 0).wait_recv()
        x_first(u, 1).wait_recv()
        merge_select(u)
        go(x_second(u, 0, 0))
        go(x_second(u, 1, 1))

    def x_step3(u):
        for right in range(2):
            for half in range(2):
                x_second(u, right, half).wait_recv()
        last_select(u)
        for dy, dc in others:
            go(a_copy(u, dy, dc))
        a_local(u).start()

    def w_start(pos):
        go(w_first(pos, 1))
        go(w_first((pos + 2) % 4, 0))

    def w_forward(pos):
        for right in (1, 0):
            unit = pos if right else (pos + 2) % 4
            w_first(unit, right).wait_recv()
            if pos < 2:
                go(w_second(unit))
            go(w_twin(unit, 3 if right else 1))

    def w_rest(n):
        for unit in (n, n + 2):
            w_second(unit).wait_recv()
            go(w_twin(unit, 2))

    def ids_ready():
        for dx in range(NX):
            for dc in range(NC):
                if dx or dc:
                    id_copy(dx, dc).wait_recv()
        copy = pltpu.make_async_copy(idv, ids_s, id_sem.at[0])
        copy.start()
        copy.wait()
        fill_table()

    def queries_ready():
        local[2].wait()
        local[3].wait()
        h_query().wait_recv()
        shift_queries()

    def blocks_ready(shared):
        for u, unit in enumerate(UNITS):
            if unit[0] == shared:
                for dy, dc in others:
                    a_copy(u, dy, dc).wait_recv()
                a_local(u).wait()

    def encode_own(stage):
        if stage == 0:
            blocks_ready(1)
            for rel in range(1, 4):
                for unit in range(4):
                    w_twin(unit, rel).wait_recv()
            for i in range(2):
                local[i].wait()
            encode_in(nbp, 2)
        elif stage == 1:
            encode_mix(2)
        else:
            encode_out(nbp, 2, [2 * y, 2 * y + 1])
            for m, right in ((0, 1), (1, 0), (1, 1), (0, 0)):
                go(e_first(m, right))

    def encode_common(i, stage):
        blocks = nbr.at[pl.ds(2 * i, 2)]
        if stage == 0:
            if i == 0:
                blocks_ready(0)
            encode_in(blocks, 2)
        elif stage == 1:
            encode_mix(2)
        else:
            encode_out(blocks, 2, [SHARED + 2 * i, SHARED + 2 * i + 1])

    def e_forward(m):
        e_first(m, 1 - m).wait_recv()
        go(e_second(m))

    def attend_step(n):
        if n == 1:
            e_first(1, 1).wait_recv()
        elif n == 2:
            e_first(0, 0).wait_recv()
        elif n == 3:
            e_second(0).wait_recv()
            e_second(1).wait_recv()
        attend((y, lax.rem(y + 3, NY), lax.rem(y + 1, NY), lax.rem(y + 2, NY), 4, 5, 6, 7)[n])

    def give_back():
        back_out[...] = out[8]
        go(h_back())

    steps = dict(
        z=z_step, zd=z_done, x1=x_step1, x2=x_step2, x3=x_step3, w0=w_start, wf=w_forward, wr=w_rest, q=queries_ready,
        qw=fold_keys, ids=ids_ready, g=greet_more, en=encode_own, er=encode_common, ef=e_forward, at=attend_step, hb=give_back,
    )
    for name, *which in ORDER:
        steps[name](*which)
    h_back().wait_recv()
    out[0] = back_in[...]
    for copy in started:
        copy.wait_send()


def fused(ids, queries, database, norm_gain, enc_qkv, enc_out, out_gain, cca_kv):
    dma = pltpu.SemaphoreType.DMA
    NU = len(UNITS)
    def per_unit(*lead):
        return [
            pltpu.VMEM(lead + (HALF, PART, WIDE * len(chunks)), BF) for _, chunks in UNITS
        ]

    scratch = [pltpu.VMEM((NZ * BLOCKS, PART, WIDE), BF) for _ in range(NF)]
    scratch += per_unit(2, 2) + per_unit(2, 2) + per_unit(2, 2, 2) + per_unit(2, 2, 2)
    scratch += [
        pltpu.VMEM((2, 2 * HALF, PART, WIDE * len(chunks)), BF) for _, chunks in UNITS
    ]
    scratch += [
        pltpu.VMEM((8, 8, 128), jnp.int32),
        pltpu.SMEM((8, 8, 128), jnp.int32),
        pltpu.SMEM((2, 8, 16), jnp.int32),
        pltpu.VMEM((EACH, ROWS, D), BF),
        pltpu.VMEM((SLOTS - SHARED, ROWS, D), BF),
        pltpu.VMEM((3, D, D), BF),
        pltpu.VMEM((D, D), BF),
        pltpu.VMEM((2, D, D), BF),
        pltpu.VMEM((SLOTS, ROWS, D), BF),
        pltpu.VMEM((8 * M, D), BF),
        pltpu.VMEM((M, D), BF),
        pltpu.VMEM((9, M, D), BF),
        pltpu.VMEM((M, D), BF),
        pltpu.VMEM((M, D), BF),
        pltpu.VMEM((2 * ROWS, D), BF),
        pltpu.VMEM((2 * ROWS, D), BF),
        pltpu.VMEM((2 * ROWS, D), F32),
        pltpu.VMEM((3, 2 * ROWS, D), BF),
        pltpu.VMEM((2 * ROWS, D), BF),
        pltpu.VMEM((8, 8 * M, D), BF),
        dma((16,)), dma((NF + 4,)), dma((NF, 8)), dma((NF, 8)), dma((NU, 6)), dma((NU, 6)),
        dma((NU, 8)), dma((NU, 8)), dma((NU,)),
        dma((12,)), dma((12,)), dma((12,)), dma((12,)), dma((6,)), dma((6,)), dma((2,)), dma((2,)),
        pltpu.SemaphoreType.REGULAR((2,)),
    ]
    vmem = pl.BlockSpec(memory_space=pltpu.VMEM)
    hbm = pl.BlockSpec(memory_space=pl.ANY)
    return pl.pallas_call(
        body,
        out_shape=jax.ShapeDtypeStruct((9, M, D), BF),
        in_specs=[vmem, hbm, hbm, vmem, hbm, hbm, vmem, hbm],
        out_specs=vmem,
        scratch_shapes=scratch,
        compiler_params=pltpu.CompilerParams(
            collective_id=0, has_side_effects=True, vmem_limit_bytes=60 * 2**20
        ),
        cost_estimate=pl.CostEstimate(flops=14 * 10**9, bytes_accessed=12 * 2**20, transcendentals=4 * 10**6),
    )(ids, queries, database, norm_gain, enc_qkv, enc_out, out_gain, cca_kv)


def per_device(queries, database, nbr_ids, norm_gain, enc_qkv, enc_out, out_gain, cca_kv):
    groups = fused(
        nbr_ids.T, queries, database, norm_gain.reshape(8, 128), enc_qkv, enc_out, out_gain.reshape(8, 128), cca_kv
    )
    tokens = queries.shape[0]
    attended = groups.reshape(9 * M, D)[1 : tokens + 1]
    unserved = (lax.axis_index("seq") == 0) & (lax.broadcasted_iota(jnp.int32, (tokens, 1), 0) < M - 1)
    return jnp.where(unserved, jnp.zeros((), BF), attended)


def solution(mesh):
    placed = (
        P(("dp", "seq"), "tensor"),
        P("seq", None, None),
        P(("dp", "seq"), None),
        P(),
        P(None, None, "tensor"),
        P("tensor", None),
        P(),
        P(None, None, "tensor"),
    )
    return jax.shard_map(
        per_device,
        mesh=mesh,
        in_specs=placed,
        out_specs=P(("dp", "seq"), "tensor"),
        check_vma=False,
    )
```
